256 devices in a mesh: rep: 8 (over x, core), fsdp: 32 (over y, z).
Axes of the slice: x: 4, y: 4, z: 8, core: 2. Of those that a mesh axis runs over, the one named last changes fastest.
Arguments:
- tokens: bfloat16 [65536, 4608], P(('rep', 'fsdp')), may hold values from -24 to 24
- cotangent: bfloat16 [65536, 1024], P(('rep', 'fsdp')), may hold values from -0.0625 to 0.0625
- weight: bfloat16 [4608, 1024], P('fsdp'), may hold values from -0.09375 to 0.09375
- momentum: float32 [8, 4608, 1024], P('rep', 'fsdp'), may hold values from -6 to 6
- lengths: int32 [256], P(('rep', 'fsdp')), may hold values from 1 to 256, as said below
- kept_index: int32 [4608, 256], P('fsdp'), may hold values from 0 to 31, as said below
Outputs:
- projected: bfloat16 [65536, 1024], P(('rep', 'fsdp'))
- new_momentum: float32 [8, 4608, 1024], P('rep', 'fsdp')
- update: float32 [4608, 1024], P('fsdp')
The draws below stay inside these ranges and needn't reach their ends.
Inputs may be any that keep to these rules, and one draw needn't show every extreme that they name: `lengths`: some sample has exactly 256 live tokens. `kept_index`: the 16 indices of one piece are distinct.
All inputs are finite; a program needn't handle non-finite values.
Results may differ from the reference program's by a relative error of at most 0.014.
Values may be sent and summed in bfloat16 or wider, within the bound.
No kernel may reach another device: no remote copies, remote signals or barrier semaphores. Data moves between devices by JAX's collectives and lax.ppermute only.
A program may use at most 128 MiB of HBM per device.

```python
import jax
import jax.numpy as jnp
from jax import lax

D = 4608
KVW = 1024
PIECE = 64
TOPK = 16
FREQ = 32
SLOT = 256
SEQ_DEV = 1
PIECES = 16
TOK_DEV = 256
SEQS = 256
TOKENS = 65536
N_REP = 8
N_FSDP = 32


def draw_lengths(key, part):
    key = jax.random.fold_in(key, 1)
    key_top, key_len, key_pos = jax.random.split(key, 3)
    ceilings = jax.random.randint(key_top, (N_REP, 1), SLOT // 4, SLOT + 1)
    drawn_lengths = 1 + jax.random.randint(key_len, (N_REP, SEQ_DEV * N_FSDP), 0, ceilings)
    flattened = drawn_lengths.reshape(SEQS)
    chosen = jax.random.randint(key_pos, (), 0, SEQS)
    return jnp.where(jnp.arange(SEQS) == chosen, SLOT, flattened).astype(jnp.int32)


def draw_kept_index(key, part):
    key = jax.random.fold_in(key, 2)
    scores = jax.random.randint(key, (D, PIECES, FREQ), 0, 2 ** 20) * FREQ + jnp.arange(FREQ)[None, None, :]
    ranked = jnp.argsort(scores, axis=-1)[:, :, :TOPK]
    return ranked.reshape(D, PIECES * TOPK).astype(jnp.int32)


def with_spikes(drawn, rng, source, target, blocks, factor):
    owner, partner = [(jnp.arange(drawn.shape[axis_at]) // (drawn.shape[axis_at] // blocks)).reshape([-1 if axis == axis_at else 1 for axis in range(drawn.ndim)]) for axis_at in (source, target)]
    chosen = jax.random.permutation(rng, blocks)[partner]
    strong = (owner == chosen) | (owner == (partner + blocks // 2) % blocks)
    return jnp.where(strong, factor * drawn, drawn)


def steps_of(own_key, dims, shards, low, top_value):
    factor_of = 1.0
    for axis_at, blocks in shards:
        steps = jax.random.uniform(jax.random.fold_in(jax.random.fold_in(own_key, 6), axis_at), (blocks,), jnp.float32, low / len(shards), top_value / len(shards))
        factor_of = factor_of * jnp.repeat(jnp.exp(steps), dims[axis_at] // blocks).reshape((-1,) + (1,) * (len(dims) - 1 - axis_at))
    return factor_of


def normal_values(stream_key, dims, deviation, most, shards=(), held_as=jnp.bfloat16):
    array = deviation * jax.random.normal(stream_key, dims, jnp.float32)
    if shards:
        array = array * steps_of(stream_key, dims, shards, -0.22, 0.18)
    return jnp.clip(array, -most, most).astype(held_as)


def bell_draw_with(stream_key, dims, scale, bound, cuts, heavy, kind=jnp.bfloat16):
    values = scale * jax.random.normal(stream_key, dims, jnp.float32)
    if cuts:
        values = values * steps_of(stream_key, dims, cuts, -0.22, 0.18)
    return jnp.clip(with_spikes(values, jax.random.fold_in(stream_key, 3), *heavy), -bound, bound).astype(kind)


def setup_inputs(seed: int = 0) -> dict:
    streams_of = jax.random.split(jax.random.key(seed), 7)
    tokens = bell_draw_with(streams_of[0], (TOKENS, D), 1.0, 24.0, ((0, 256),), (0, 1, 256, 6.0))
    cotangent = normal_values(streams_of[1], (TOKENS, KVW), (TOK_DEV * N_FSDP) ** -0.5, 0.0625, ((0, 256),))
    weight = normal_values(streams_of[2], (D, KVW), D ** -0.5, 0.09375, ((0, 32),))
    momentum = normal_values(streams_of[3], (N_REP, D, KVW), 1.0, 6.0, ((0, 8), (1, 32)), jnp.float32)
    lengths = draw_lengths(jax.random.fold_in(streams_of[6], 71), 0)
    kept_index = draw_kept_index(jax.random.fold_in(streams_of[6], 71), 0)
    return dict(tokens=tokens, cotangent=cotangent, weight=weight, momentum=momentum, lengths=lengths, kept_index=kept_index)


def dct_matrix():
    frequency = jnp.arange(PIECE)[:, None].astype(jnp.float32)
    position = jnp.arange(PIECE)[None, :].astype(jnp.float32)
    norm_scale = jnp.where(frequency == 0.0, jnp.sqrt(1.0 / PIECE), jnp.sqrt(2.0 / PIECE))
    return norm_scale * jnp.cos(jnp.pi * (2.0 * position + 1.0) * frequency / (2.0 * PIECE))

def reference(tokens, cotangent, weight, momentum, lengths, kept_index):
    projected = jnp.dot(tokens, weight, preferred_element_type=jnp.float32).astype(jnp.bfloat16)
    group_rows = TOK_DEV * N_FSDP
    live_mask = jnp.arange(SLOT)[None, :] < lengths[:, None]
    masked = cotangent.reshape(SEQS, SLOT, KVW) * live_mask[:, :, None].astype(cotangent.dtype)
    masked = masked.reshape(N_REP, group_rows, KVW)
    grouped = tokens.reshape(N_REP, group_rows, D)

    def one_group(pair):
        group_tokens, group_masked = pair
        return lax.dot_general(group_tokens, group_masked, (((0,), (0,)), ((), ())), preferred_element_type=jnp.float32)
    grad = lax.map(one_group, (grouped, masked))
    blended = 0.9 * momentum + grad
    dct_table = dct_matrix()
    highest = lax.Precision.HIGHEST
    coeffs = jnp.einsum('rdpn,kn->rdpk', blended.reshape(N_REP, D, PIECES, PIECE), dct_table, precision=highest)
    kept = kept_index.reshape(D, PIECES, TOPK)
    values = jnp.take_along_axis(coeffs, jnp.broadcast_to(kept[None], (N_REP, D, PIECES, TOPK)), axis=3)
    selector = (kept[:, :, :, None] == jnp.arange(PIECE)[None, None, None, :]).astype(jnp.float32)
    dense_coeffs = jnp.einsum('rdpj,dpjk->rdpk', values, selector, precision=highest)
    rebuilt = jnp.einsum('rdpk,kn->rdpn', dense_coeffs, dct_table, precision=highest).reshape(N_REP, D, KVW)
    new_momentum = blended - rebuilt
    update = lax.optimization_barrier(jnp.sum(rebuilt, axis=0))
    return (projected, new_momentum, update)
```

```python
import functools

import jax
import jax.numpy as jnp
import numpy as np
from jax import lax
from jax.experimental import pallas as pl
from jax.experimental.pallas import tpu as pltpu
from jax.sharding import Mesh, PartitionSpec as P

PIECE = 64
TOPK = 16
FREQ = 32
SLOT = 256
GROUP = 128 // FREQ * PIECE

BF16 = jnp.bfloat16
F32 = jnp.float32
HIGHEST = lax.Precision.HIGHEST
VMEM = pl.BlockSpec(memory_space=pltpu.VMEM)
SMEM = pl.BlockSpec(memory_space=pltpu.SMEM)
ANY = pl.BlockSpec(memory_space=pl.ANY)
PARAMS = pltpu.CompilerParams(vmem_limit_bytes=40 * 1024 * 1024)


def group_table():
    k = np.arange(FREQ)[:, None].astype(np.float64)
    n = np.arange(PIECE)[None, :].astype(np.float64)
    scale = np.where(k == 0, np.sqrt(1.0 / PIECE), np.sqrt(2.0 / PIECE))
    rows = scale * np.cos(np.pi * (2 * n + 1) * k / (2 * PIECE))
    return jnp.asarray(np.kron(np.eye(GROUP // PIECE), rows.T), F32)


def spread_table(pieces):
    table = np.zeros((TOPK, pieces * TOPK, pieces * FREQ), np.float32)
    for j in range(TOPK):
        for p in range(pieces):
            table[j, p * TOPK + j, p * FREQ : (p + 1) * FREQ] = 1.0
    return jnp.asarray(table, BF16)


def split_kernel(y_ref, tok_ref, *rest):
    outs, sems = rest[:-1], rest[-1]
    width = outs[0].shape[1]
    copies = []
    for d, out in enumerate(outs):
        start = pl.multiple_of(lax.bitwise_xor(y_ref[0], d) * width, width)
        copies.append(pltpu.make_async_copy(tok_ref.at[:, pl.ds(start, width)], out, sems.at[d]))
    for copy in copies:
        copy.start()
    for copy in copies:
        copy.wait()


def split_tokens(y, tokens, ny):
    rows, width = tokens.shape[0], tokens.shape[1] // ny
    return pl.pallas_call(
        split_kernel,
        out_shape=[jax.ShapeDtypeStruct((rows, width), BF16)] * ny,
        in_specs=[SMEM, ANY],
        out_specs=[ANY] * ny,
        scratch_shapes=[pltpu.SemaphoreType.DMA((ny,))],
    )(y, tokens)


def contract_rows(left, right):
    return lax.dot_general(left, right, (((0,), (0,)), ((), ())), preferred_element_type=F32)


def grad_kernel(ny, nz, z_ref, *rest):
    toks, cots = rest[:ny], rest[ny : 2 * ny]
    outs, acc = rest[2 * ny : 2 * ny + nz], rest[-1]
    acc[...] = contract_rows(toks[0][...], cots[0][...])
    for tok, cot in zip(toks[1:], cots[1:]):
        acc[...] += contract_rows(tok[...], cot[...])
    rows = outs[0].shape[0]
    for k, out in enumerate(outs):
        block = lax.rem(z_ref[0] + k, nz)
        start = pl.multiple_of(block * rows, 16)
        out[...] = acc[pl.ds(start, rows), :].astype(out.dtype)


def grad_blocks(z, toks, cots, nz):
    ny = len(toks)
    depth, width = toks[0].shape[1], cots[0].shape[1]
    rows = depth // nz
    return pl.pallas_call(
        functools.partial(grad_kernel, ny, nz),
        out_shape=[jax.ShapeDtypeStruct((rows, width), F32 if k == 0 else BF16) for k in range(nz)],
        in_specs=[SMEM] + [VMEM] * (2 * ny),
        out_specs=[VMEM] * nz,
        scratch_shapes=[pltpu.VMEM((depth, width), F32)],
        compiler_params=PARAMS,
    )(z, *toks, *cots)


def keep_kernel(kept_ref, spread_ref, keep_ref):
    kept = kept_ref[...].astype(F32).astype(BF16)
    shape = keep_ref.shape
    freq = lax.rem(lax.broadcasted_iota(jnp.int32, shape, 1), FREQ).astype(F32)
    keep = jnp.zeros(shape, F32)
    for j in range(TOPK):
        index = jnp.dot(kept, spread_ref[j], preferred_element_type=F32)
        keep = jnp.where(index == freq, 1.0, keep)
    keep_ref[...] = keep


def keep_mask(kept_index):
    rows, slots = kept_index.shape
    pieces = slots // TOPK
    return pl.pallas_call(
        keep_kernel,
        out_shape=jax.ShapeDtypeStruct((rows, pieces * FREQ), F32),
        in_specs=[VMEM] * 2,
        out_specs=VMEM,
        compiler_params=PARAMS,
    )(kept_index, spread_table(pieces))


def encode_kernel(momentum_ref, keep_ref, table_ref, table_t_ref, own_ref, *rest):
    parts, (new_ref, coeff_ref) = rest[:-2], rest[-2:]
    width = parts[0].shape[1]
    halves = momentum_ref.shape[1] // width
    for h in range(halves):
        cols = slice(h * width, (h + 1) * width)
        grad = own_ref[:, cols]
        for part in parts[h::halves]:
            grad = grad + part[...].astype(F32)
        new_ref[:, cols] = 0.9 * momentum_ref[:, cols] + grad
    for g in range(momentum_ref.shape[1] // GROUP):
        cols = slice(g * GROUP, (g + 1) * GROUP)
        lanes = slice(g * 128, (g + 1) * 128)
        blended = new_ref[:, cols]
        coeffs = jnp.dot(blended, table_ref[...], precision=HIGHEST, preferred_element_type=F32)
        coeffs = coeffs * keep_ref[:, lanes]
        coeff_ref[:, lanes] = coeffs.astype(BF16)
        rebuilt = jnp.dot(coeffs, table_t_ref[...], precision=HIGHEST, preferred_element_type=F32)
        new_ref[:, cols] = blended - rebuilt


def encode(momentum, keep, table, own, parts):
    return pl.pallas_call(
        encode_kernel,
        out_shape=[
            jax.ShapeDtypeStruct(momentum.shape, F32),
            jax.ShapeDtypeStruct(keep.shape, BF16),
        ],
        in_specs=[VMEM] * (5 + len(parts)),
        out_specs=[VMEM] * 2,
        compiler_params=PARAMS,
    )(momentum, keep, table, table.T, own, *parts)


def decode_kernel(mine_ref, other_ref, table_t_ref, update_ref):
    for g in range(update_ref.shape[1] // GROUP):
        lanes = slice(g * 128, (g + 1) * 128)
        coeffs = mine_ref[:, lanes] + other_ref[:, lanes]
        update_ref[:, g * GROUP : (g + 1) * GROUP] = jnp.dot(
            coeffs, table_t_ref[...], precision=HIGHEST, preferred_element_type=F32
        )


def decode(mine, other, table, width):
    return pl.pallas_call(
        decode_kernel,
        out_shape=jax.ShapeDtypeStruct((mine.shape[0], width), F32),
        in_specs=[VMEM] * 3,
        out_specs=VMEM,
        compiler_params=PARAMS,
    )(mine, other, table.T)


def swap(array, axis, d):
    return lax.ppermute(array, axis, [(i, i ^ d) for i in range(lax.axis_size(axis))])


def shift(array, axis, d):
    size = lax.axis_size(axis)
    return lax.ppermute(array, axis, [(i, (i + d) % size) for i in range(size)])


def reduce_ring(blocks):
    nz = len(blocks)
    width = blocks[0].shape[1] // 2
    parts = []
    for sign in (1, -1):
        for h in range(2):
            cols = slice(h * width, (h + 1) * width)
            far = nz // 2 if (sign == 1) == (h == 0) else nz // 2 - 1
            moving = blocks[sign * far % nz][:, cols]
            for k in range(far - 1, -1, -1):
                moving = shift(moving, "z", sign)
                if k:
                    own = blocks[sign * k % nz][:, cols]
                    moving = (moving.astype(F32) + own.astype(F32)).astype(BF16)
            parts.append(moving)
    return parts


def per_device(tokens, cotangent, weight, momentum, lengths, kept_index):
    ny, nz = lax.axis_size("y"), lax.axis_size("z")
    y = lax.axis_index("y").astype(jnp.int32).reshape(1)
    z = lax.axis_index("z").astype(jnp.int32).reshape(1)
    core = lax.axis_index("core")
    width = weight.shape[1]
    half = width // 2

    weight_half = lax.dynamic_slice_in_dim(weight, core * half, half, axis=1)
    weight_mine = lax.all_gather(weight_half, "z", axis=0, tiled=True)

    live = lax.broadcasted_iota(jnp.int32, (lengths.shape[0], SLOT), 1) < lengths[:, None]
    masked = cotangent * live.reshape(-1, 1).astype(BF16)
    toks = split_tokens(y, tokens, ny)
    toks = [toks[0]] + [swap(toks[d], "y", d) for d in range(1, ny)]
    cots = [masked] + [swap(masked, "y", d) for d in range(1, ny)]

    weight_other = swap(weight_mine, "core", 1)
    weight_quarter = jnp.where(
        core == 0,
        jnp.concatenate([weight_mine, weight_other], axis=1),
        jnp.concatenate([weight_other, weight_mine], axis=1),
    )

    blocks = grad_blocks(z, toks, cots, nz)
    parts = reduce_ring(blocks)

    total = jnp.dot(toks[0], weight_quarter, preferred_element_type=F32)
    sent = [jnp.dot(toks[d], weight_quarter, preferred_element_type=F32).astype(BF16) for d in range(1, ny)]
    for d in range(1, ny):
        total = total + swap(sent[d - 1], "y", d).astype(F32)
    projected = total.astype(BF16)

    table = group_table()
    keep = keep_mask(kept_index)
    new_momentum, coeffs = encode(momentum[0], keep, table, blocks[0], parts)
    one, two, three = (swap(coeffs, "x", d).astype(F32) for d in (1, 2, 3))
    mine = (coeffs.astype(F32) + one) + (two + three)
    other = swap(mine, "core", 1)
    update = decode(mine, other, table, width)
    return (projected, new_momentum[None], update)


def solution(mesh):
    fine = Mesh(mesh.devices.reshape(4, 2, 4, 8), ("x", "core", "y", "z"))
    rep, fsdp = ("x", "core"), ("y", "z")
    placed = (
        P(rep + fsdp, None),
        P(rep + fsdp, None),
        P(fsdp, None),
        P(rep, fsdp, None),
        P(rep + fsdp),
        P(fsdp, None),
    )
    return jax.shard_map(
        per_device,
        mesh=fine,
        in_specs=placed,
        out_specs=(P(rep + fsdp, None), P(rep, fsdp, None), P(fsdp, None)),
        check_vma=False,
    )
```

```python
import functools

import jax
import jax.numpy as jnp
import numpy as np
from jax import lax
from jax.experimental import pallas as pl
from jax.experimental.pallas import tpu as pltpu
from jax.sharding import Mesh, PartitionSpec as P

PIECE = 64
TOPK = 16
FREQ = 32
SLOT = 256
GROUP = 128 // FREQ * PIECE

BF16 = jnp.bfloat16
F32 = jnp.float32
HIGHEST = lax.Precision.HIGHEST
VMEM = pl.BlockSpec(memory_space=pltpu.VMEM)
SMEM = pl.BlockSpec(memory_space=pltpu.SMEM)
PARAMS = pltpu.CompilerParams(vmem_limit_bytes=14 * 1024 * 1024)


def group_table():
    k = np.arange(FREQ)[:, None].astype(np.float64)
    n = np.arange(PIECE)[None, :].astype(np.float64)
    scale = np.where(k == 0, np.sqrt(1.0 / PIECE), np.sqrt(2.0 / PIECE))
    rows = scale * np.cos(np.pi * (2 * n + 1) * k / (2 * PIECE))
    return jnp.asarray(np.kron(np.eye(GROUP // PIECE), rows.T), F32)


def split_kernel(y_ref, length_ref, tok_ref, cot_ref, *outs):
    cols = cot_ref.shape[1]
    width = outs[0].shape[1] - cols
    position = lax.broadcasted_iota(jnp.int32, cot_ref.shape, 0)
    masked = jnp.where(position < length_ref[0], cot_ref[...], jnp.zeros_like(cot_ref))
    for d, out in enumerate(outs):
        start = pl.multiple_of(lax.bitwise_xor(y_ref[0], d) * width, width)
        out[:, :width] = tok_ref[:, pl.ds(start, width)]
        out[:, width:] = masked


def split_inputs(y, lengths, tokens, cotangent, ny):
    rows, width = tokens.shape[0], tokens.shape[1] // ny
    shape = (rows, width + cotangent.shape[1])
    return pl.pallas_call(
        split_kernel,
        out_shape=[jax.ShapeDtypeStruct(shape, BF16)] * ny,
        in_specs=[SMEM, SMEM, VMEM, VMEM],
        out_specs=[VMEM] * ny,
        compiler_params=PARAMS,
    )(y, lengths, tokens, cotangent)


def contract_rows(left, right):
    return lax.dot_general(left, right, (((0,), (0,)), ((), ())), preferred_element_type=F32)


def grad_kernel(nz, width, z_ref, *refs):
    mixed, outs, acc = refs[:-8], refs[-8:-1], refs[-1]
    for d, both in enumerate(mixed):
        term = contract_rows(both[:, :width], both[:, width:])
        acc[...] = acc[...] + term if d else term

    rows = width // nz
    half = acc.shape[1] // 2
    left, right = slice(0, half), slice(half, 2 * half)

    def block(k, cols=slice(None)):
        at = lax.rem(z_ref[0] + k % nz, nz)
        return acc[pl.ds(pl.multiple_of(at * rows, 16), rows), cols]

    own, up, down, far_up, far_down, ahead, behind = outs
    own[...] = block(0)
    up[0] = block(1).astype(BF16)
    up[1] = block(3).astype(BF16)
    down[0] = block(-1).astype(BF16)
    down[1] = block(-3).astype(BF16)
    far_up[...] = block(4, left).astype(BF16)
    far_down[...] = block(-4, right).astype(BF16)
    ahead[...] = block(2).astype(BF16)
    behind[...] = block(-2).astype(BF16)


def grad_terms(z, mixed, nz, cols):
    width = mixed[0].shape[1] - cols
    rows = width // nz
    shapes = [((rows, cols), F32)] + [
        (shape, BF16) for shape in [(2, rows, cols)] * 2 + [(rows, cols // 2)] * 2 + [(rows, cols)] * 2
    ]
    return pl.pallas_call(
        functools.partial(grad_kernel, nz, width),
        out_shape=[jax.ShapeDtypeStruct(*shape) for shape in shapes],
        in_specs=[SMEM] + [VMEM] * len(mixed),
        out_specs=[VMEM] * len(shapes),
        scratch_shapes=[pltpu.VMEM((width, cols), F32)],
        compiler_params=pltpu.CompilerParams(vmem_limit_bytes=24 * 1024 * 1024),
    )(z, *mixed)


def relay_kernel(ahead_ref, behind_ref, up_ref, down_ref, far_up_ref, far_down_ref, ahead_out, behind_out):
    half = far_up_ref.shape[1]
    for near, pair, far, out, far_cols in (
        (ahead_ref, up_ref, far_up_ref, ahead_out, slice(0, half)),
        (behind_ref, down_ref, far_down_ref, behind_out, slice(half, 2 * half)),
    ):
        total = near[...].astype(F32) + pair[1].astype(F32)
        out[...] = total.astype(BF16)
        out[:, far_cols] = (total[:, far_cols] + far[...].astype(F32)).astype(BF16)


def relay(*terms):
    shape = jax.ShapeDtypeStruct(terms[0].shape, BF16)
    return pl.pallas_call(
        relay_kernel,
        out_shape=[shape, shape],
        in_specs=[VMEM] * len(terms),
        out_specs=[VMEM] * 2,
        compiler_params=PARAMS,
    )(*terms)


def project_kernel(width, first_ref, second_ref, weight_ref, out_ref):
    rows = first_ref.shape[0]
    for i, tok in enumerate((first_ref, second_ref)):
        out_ref[pl.ds(i * rows, rows), :] = jnp.dot(
            tok[:, :width], weight_ref[...], preferred_element_type=F32
        ).astype(BF16)


def project_last_kernel(width, y_ref, first_ref, second_ref, weight_ref, done_ref, out_ref):
    rows = first_ref.shape[0]

    def store(d, value):
        start = pl.multiple_of(lax.bitwise_xor(y_ref[0], d) * rows, rows)
        out_ref[pl.ds(start, rows), :] = value

    for d in range(2):
        store(d, done_ref[d * rows : (d + 1) * rows, :])
    for d, tok in ((2, first_ref), (3, second_ref)):
        store(d, jnp.dot(tok[:, :width], weight_ref[...], preferred_element_type=F32).astype(BF16))


def project_terms(y, mixed, weight):
    rows, depth = mixed[0].shape[0], weight.shape[0]
    done = pl.pallas_call(
        functools.partial(project_kernel, depth),
        out_shape=jax.ShapeDtypeStruct((2 * rows, weight.shape[1]), BF16),
        in_specs=[VMEM] * 3,
        out_specs=VMEM,
        compiler_params=PARAMS,
    )(mixed[0], mixed[1], weight)
    return pl.pallas_call(
        functools.partial(project_last_kernel, depth),
        out_shape=jax.ShapeDtypeStruct((4 * rows, weight.shape[1]), BF16),
        in_specs=[SMEM] + [VMEM] * 4,
        out_specs=VMEM,
        compiler_params=PARAMS,
    )(y, mixed[2], mixed[3], weight, done)


def keep_kernel(kept_ref, keep_ref):
    kept = kept_ref[...].astype(F32).astype(BF16)
    rows, lanes = keep_ref.shape
    freq = lax.rem(lax.broadcasted_iota(jnp.int32, (rows, lanes), 1), FREQ).astype(F32)
    slot = lax.broadcasted_iota(jnp.int32, (kept.shape[1], lanes), 0)
    first = lax.broadcasted_iota(jnp.int32, (kept.shape[1], lanes), 1) // FREQ * TOPK
    keep = jnp.zeros((rows, lanes), F32)
    for j in range(TOPK):
        spread = (slot == first + j).astype(F32).astype(BF16)
        index = jnp.dot(kept, spread, preferred_element_type=F32)
        keep = jnp.where(index == freq, 1.0, keep)
    keep_ref[...] = keep


def keep_mask(kept_index):
    rows, slots = kept_index.shape
    return pl.pallas_call(
        keep_kernel,
        out_shape=jax.ShapeDtypeStruct((rows, slots // TOPK * FREQ), F32),
        in_specs=[VMEM],
        out_specs=VMEM,
        compiler_params=PARAMS,
    )(kept_index)


def encode_kernel(momentum_ref, keep_ref, table_ref, table_t_ref, own_ref, up_ref, down_ref, ahead_ref, behind_ref, new_ref, coeff_ref):
    for g in range(momentum_ref.shape[1] // GROUP):
        cols = slice(g * GROUP, (g + 1) * GROUP)
        lanes = slice(g * 128, (g + 1) * 128)
        grad = own_ref[:, cols] + up_ref[0, :, cols].astype(F32) + down_ref[0, :, cols].astype(F32)
        grad = grad + ahead_ref[:, cols].astype(F32) + behind_ref[:, cols].astype(F32)
        blended = 0.9 * momentum_ref[:, cols] + grad
        coeffs = jnp.dot(blended, table_ref[...], precision=HIGHEST, preferred_element_type=F32)
        coeffs = coeffs * keep_ref[:, lanes]
        coeff_ref[:, lanes] = coeffs.astype(BF16)
        rebuilt = jnp.dot(coeffs, table_t_ref[...], precision=HIGHEST, preferred_element_type=F32)
        new_ref[:, cols] = blended - rebuilt


def encode(momentum, keep, table, grads):
    return pl.pallas_call(
        encode_kernel,
        out_shape=[
            jax.ShapeDtypeStruct(momentum.shape, F32),
            jax.ShapeDtypeStruct(keep.shape, BF16),
        ],
        in_specs=[VMEM] * (4 + len(grads)),
        out_specs=[VMEM] * 2,
        compiler_params=PARAMS,
    )(momentum, keep, table, table.T, *grads)


def decode_kernel(mine_ref, other_ref, table_t_ref, update_ref):
    for g in range(update_ref.shape[1] // GROUP):
        lanes = slice(g * 128, (g + 1) * 128)
        coeffs = mine_ref[:, lanes] + other_ref[:, lanes]
        update_ref[:, g * GROUP : (g + 1) * GROUP] = jnp.dot(
            coeffs, table_t_ref[...], precision=HIGHEST, preferred_element_type=F32
        )


def decode(mine, other, table, width):
    return pl.pallas_call(
        decode_kernel,
        out_shape=jax.ShapeDtypeStruct((mine.shape[0], width), F32),
        in_specs=[VMEM] * 3,
        out_specs=VMEM,
        compiler_params=PARAMS,
    )(mine, other, table.T)


def swap(array, axis, d):
    return lax.ppermute(array, axis, [(i, i ^ d) for i in range(lax.axis_size(axis))])


def shift(array, axis, d):
    size = lax.axis_size(axis)
    return lax.ppermute(array, axis, [(i, (i + d) % size) for i in range(size)])


def reduce_over_z(own, up, down, far_up, far_down, ahead, behind):
    up, down = shift(up, "z", 1), shift(down, "z", -1)
    far_up, far_down = shift(far_up, "z", 2), shift(far_down, "z", -2)
    ahead, behind = relay(ahead, behind, up, down, far_up, far_down)
    return own, up, down, shift(ahead, "z", 2), shift(behind, "z", -2)


def per_device(tokens, cotangent, weight, momentum, lengths, kept_index):
    ny, nz = lax.axis_size("y"), lax.axis_size("z")
    y = lax.axis_index("y").astype(jnp.int32).reshape(1)
    z = lax.axis_index("z").astype(jnp.int32).reshape(1)
    width = weight.shape[1]

    weight_quarter = lax.all_gather(weight, "z", axis=0, tiled=True)
    mixed = split_inputs(y, lengths, tokens, cotangent, ny)
    mixed = [mixed[0]] + [swap(mixed[d], "y", d) for d in range(1, ny)]

    terms = grad_terms(z, mixed, nz, width)
    grads = reduce_over_z(*terms)
    partial = project_terms(y, mixed, weight_quarter)
    projected = lax.psum_scatter(partial, "y", scatter_dimension=0, tiled=True)

    table = group_table()
    new_momentum, coeffs = encode(momentum[0], keep_mask(kept_index), table, grads)
    one, two, three = (swap(coeffs, "x", d).astype(F32) for d in (1, 2, 3))
    mine = (coeffs.astype(F32) + one) + (two + three)
    update = decode(mine, swap(mine, "core", 1), table, width)
    return (projected, new_momentum[None], update)


def solution(mesh):
    fine = Mesh(mesh.devices.reshape(4, 2, 4, 8), ("x", "core", "y", "z"))
    rep, fsdp = ("x", "core"), ("y", "z")
    placed = (
        P(rep + fsdp, None),
        P(rep + fsdp, None),
        P(fsdp, None),
        P(rep, fsdp, None),
        P(rep + fsdp),
        P(fsdp, None),
    )
    return jax.shard_map(
        per_device,
        mesh=fine,
        in_specs=placed,
        out_specs=(P(rep + fsdp, None), P(rep, fsdp, None), P(fsdp, None)),
        check_vma=False,
    )
```

```python
import functools

import jax
import jax.numpy as jnp
import numpy as np
from jax import lax
from jax.experimental import pallas as pl
from jax.experimental.pallas import tpu as pltpu
from jax.sharding import Mesh, PartitionSpec as P

PIECE = 64
TOPK = 16
FREQ = 32
SLOT = 256
GROUP = 128 // FREQ * PIECE

HALVES = 2

BF16 = jnp.bfloat16
F32 = jnp.float32
HIGHEST = lax.Precision.HIGHEST
VMEM = pl.BlockSpec(memory_space=pltpu.VMEM)
SMEM = pl.BlockSpec(memory_space=pltpu.SMEM)
HBM = pl.BlockSpec(memory_space=pltpu.HBM)
PARAMS = pltpu.CompilerParams(vmem_limit_bytes=14 * 1024 * 1024)
ALL = pltpu.CompilerParams(vmem_limit_bytes=56 * 1024 * 1024)
BIG = pltpu.CompilerParams(vmem_limit_bytes=28 * 1024 * 1024)


def group_table():
    k = np.arange(FREQ)[:, None].astype(np.float64)
    n = np.arange(PIECE)[None, :].astype(np.float64)
    scale = np.where(k == 0, np.sqrt(1.0 / PIECE), np.sqrt(2.0 / PIECE))
    rows = scale * np.cos(np.pi * (2 * n + 1) * k / (2 * PIECE))
    return jnp.asarray(np.kron(np.eye(GROUP // PIECE), rows.T), F32)


def mask_rows(cot, length):
    position = lax.broadcasted_iota(jnp.int32, cot.shape, 0)
    return jnp.where(position < length, cot, jnp.zeros_like(cot))


def split_kernel(order, y_ref, length_ref, tok_ref, cot_ref, *refs):
    count = len(order)
    outs, bufs, (cot_buffer, in_sems, out_sems) = refs[:count], refs[count : 2 * count], refs[2 * count :]
    width = outs[0].shape[1] - cot_ref.shape[1]
    cot_copy = pltpu.make_async_copy(cot_ref, cot_buffer, in_sems.at[count])
    cot_copy.start()
    in_copies, out_copies = [], []
    for i, d in enumerate(order):
        start = pl.multiple_of(lax.bitwise_xor(y_ref[0], d) * width, width)
        copy = pltpu.make_async_copy(tok_ref.at[:, pl.ds(start, width)], bufs[i].at[:, :width], in_sems.at[i])
        copy.start()
        in_copies.append(copy)
        out_copies.append(pltpu.make_async_copy(bufs[i], outs[i], out_sems.at[i]))
    cot_copy.wait()
    masked = mask_rows(cot_buffer[...], length_ref[0])
    for buf, in_copy, out_copy in zip(bufs, in_copies, out_copies):
        buf[:, width:] = masked
        in_copy.wait()
        out_copy.start()
    for copy in out_copies:
        copy.wait()


def split_inputs(y, lengths, tokens, cotangent, ny, order):
    rows, width = tokens.shape[0], tokens.shape[1] // ny
    shape = (rows, width + cotangent.shape[1])
    count = len(order)
    return pl.pallas_call(
        functools.partial(split_kernel, order),
        out_shape=[jax.ShapeDtypeStruct(shape, BF16)] * count,
        in_specs=[SMEM, SMEM] + [HBM] * 2,
        out_specs=[pl.BlockSpec(memory_space=pl.ANY)] * count,
        scratch_shapes=[pltpu.VMEM(shape, BF16)] * count
        + [
            pltpu.VMEM(cotangent.shape, BF16),
            pltpu.SemaphoreType.DMA((count + 1,)),
            pltpu.SemaphoreType.DMA((count,)),
        ],
        compiler_params=ALL,
    )(y, lengths, tokens, cotangent)


def whole(array):
    return pl.BlockSpec(array.shape, lambda i, *scalars: (0,) * array.ndim)


def own_columns(tokens, ny):
    return pl.BlockSpec((tokens.shape[0], tokens.shape[1] // ny), lambda i, y, *scalars: (0, y[0]))


def contract_rows(left, right):
    return lax.dot_general(left, right, (((0,), (0,)), ((), ())), preferred_element_type=F32)


def grad_first_kernel(y_ref, length_ref, own_ref, cot_ref, both_ref, after_ref, acc_ref):
    width = own_ref.shape[1]
    acc_ref[...] = contract_rows(own_ref[...], mask_rows(cot_ref[...], length_ref[0]))
    acc_ref[...] = acc_ref[...] + contract_rows(both_ref[:, :width], both_ref[:, width:])


def grad_first(y, lengths, tokens, cotangent, both, ny, after):
    shape = (tokens.shape[1] // ny, cotangent.shape[1])
    return pl.pallas_call(
        grad_first_kernel,
        out_shape=jax.ShapeDtypeStruct(shape, F32),
        grid_spec=pltpu.PrefetchScalarGridSpec(
            num_scalar_prefetch=2,
            grid=(1,),
            in_specs=[
                own_columns(tokens, ny),
                whole(cotangent),
                whole(both),
                pl.BlockSpec(memory_space=pl.ANY),
            ],
            out_specs=pl.BlockSpec(shape, lambda i, *scalars: (0, 0)),
        ),
        compiler_params=BIG,
    )(y, lengths, tokens, cotangent, both, after)


def grad_kernel(nz, skip, place_ref, first_ref, one_ref, two_ref, *refs):
    outs, acc = refs[skip:-1], refs[-1]
    width = first_ref.shape[0]
    acc[...] = first_ref[...] + contract_rows(one_ref[:, :width], one_ref[:, width:])
    acc[...] = acc[...] + contract_rows(two_ref[:, :width], two_ref[:, width:])

    rows = width // nz
    z, side = place_ref[0], place_ref[1]
    halves = len(outs) // 2
    cols = acc.shape[1] // halves

    def block(k, h):
        at = lax.rem(z + k * side + nz, nz)
        return acc[pl.ds(pl.multiple_of(at * rows, 16), rows), h * cols : (h + 1) * cols]

    for h in range(halves):
        kept, given = outs[2 * h : 2 * h + 2]
        for j in range(nz // 2):
            kept[j] = block(j, h)
            given[j] = block(-1 - j, h).astype(BF16)


def grad_terms(place, first, one, two, nz, halves, after):
    width, cols = first.shape
    shape = (nz // 2, width // nz, cols // halves)
    return pl.pallas_call(
        functools.partial(grad_kernel, nz, len(after)),
        out_shape=[jax.ShapeDtypeStruct(shape, F32), jax.ShapeDtypeStruct(shape, BF16)] * halves,
        in_specs=[SMEM] + [VMEM] * 3 + [pl.BlockSpec(memory_space=pl.ANY)] * len(after),
        out_specs=[VMEM] * (2 * halves),
        scratch_shapes=[pltpu.VMEM((width, cols), F32)],
        compiler_params=BIG,
    )(place, first, one, two, *after)


def relay_kernel(kept_ref, got_ref, *rest):
    near_ref, far_ref = rest[-2:]
    for j in range(2):
        near_ref[j] = kept_ref[j] + got_ref[j].astype(F32)
        far_ref[j] = (kept_ref[j + 2] + got_ref[j + 2].astype(F32)).astype(BF16)


def relay(kept, got, after):
    shape = (2, *kept.shape[1:])
    return pl.pallas_call(
        relay_kernel,
        out_shape=[jax.ShapeDtypeStruct(shape, F32), jax.ShapeDtypeStruct(shape, BF16)],
        in_specs=[VMEM] * 2 + [pl.BlockSpec(memory_space=pl.ANY)] * len(after),
        out_specs=[VMEM] * 2,
        compiler_params=PARAMS,
    )(kept, got, *after)


def project_first_kernel(y_ref, own_ref, both_ref, weight_ref, total_ref, out_ref):
    width = own_ref.shape[1]
    total_ref[...] = jnp.dot(own_ref[...], weight_ref[...], preferred_element_type=F32)
    out_ref[...] = jnp.dot(both_ref[:, :width], weight_ref[...], preferred_element_type=F32).astype(BF16)


def project_first(y, tokens, both, weight, ny):
    shape = (tokens.shape[0], weight.shape[1])
    return pl.pallas_call(
        project_first_kernel,
        out_shape=[jax.ShapeDtypeStruct(shape, F32), jax.ShapeDtypeStruct(shape, BF16)],
        grid_spec=pltpu.PrefetchScalarGridSpec(
            num_scalar_prefetch=1,
            grid=(1,),
            in_specs=[own_columns(tokens, ny), whole(both), whole(weight)],
            out_specs=[pl.BlockSpec(shape, lambda i, y: (0, 0))] * 2,
        ),
        compiler_params=BIG,
    )(y, tokens, both, weight)


def project_kernel(one_ref, two_ref, weight_ref, one_out, two_out):
    width = weight_ref.shape[0]
    for both, out in ((one_ref, one_out), (two_ref, two_out)):
        out[...] = jnp.dot(both[:, :width], weight_ref[...], preferred_element_type=F32).astype(BF16)


def project_rest(one, two, weight):
    shape = jax.ShapeDtypeStruct((one.shape[0], weight.shape[1]), BF16)
    return pl.pallas_call(
        project_kernel,
        out_shape=[shape, shape],
        in_specs=[VMEM] * 3,
        out_specs=[VMEM] * 2,
        compiler_params=PARAMS,
    )(one, two, weight)


def keep_kernel(kept_ref, keep_ref):
    kept = kept_ref[...].astype(F32).astype(BF16)
    rows, lanes = keep_ref.shape
    freq = lax.rem(lax.broadcasted_iota(jnp.int32, (rows, lanes), 1), FREQ).astype(F32)
    slot = lax.broadcasted_iota(jnp.int32, (kept.shape[1], lanes), 0)
    first = lax.broadcasted_iota(jnp.int32, (kept.shape[1], lanes), 1) // FREQ * TOPK
    keep = jnp.zeros((rows, lanes), F32)
    for j in range(TOPK):
        spread = (slot == first + j).astype(F32).astype(BF16)
        index = jnp.dot(kept, spread, preferred_element_type=F32)
        keep = jnp.where(index == freq, 1.0, keep)
    keep_ref[...] = keep


def keep_mask(kept_index):
    rows, slots = kept_index.shape
    return pl.pallas_call(
        keep_kernel,
        out_shape=jax.ShapeDtypeStruct((rows, slots // TOPK * FREQ), F32),
        in_specs=[VMEM],
        out_specs=VMEM,
        compiler_params=PARAMS,
    )(kept_index)


def encode_kernel(start, momentum_ref, keep_ref, table_ref, near_ref, far_ref, last_ref, *rest):
    blended_ref, coeff_ref, sent_ref = rest[-3:]
    for g in range(blended_ref.shape[1] // GROUP):
        cols = slice(g * GROUP, (g + 1) * GROUP)
        lanes = slice(g * 128, (g + 1) * 128)
        at = start + g * GROUP
        grad = near_ref[0, :, cols] + far_ref[0, :, cols].astype(F32) + last_ref[:, cols].astype(F32)
        blended = 0.9 * momentum_ref[:, at : at + GROUP] + grad
        coeffs = jnp.dot(blended, table_ref[...], precision=HIGHEST, preferred_element_type=F32)
        at = at // GROUP * 128
        coeffs = coeffs * keep_ref[:, at : at + 128]
        blended_ref[:, cols] = blended
        coeff_ref[:, lanes] = coeffs
        sent_ref[:, lanes] = coeffs.astype(BF16)


def encode(start, momentum, keep, table, grads, after):
    rows, cols = grads[2].shape
    lanes = cols // GROUP * 128
    return pl.pallas_call(
        functools.partial(encode_kernel, start),
        out_shape=[
            jax.ShapeDtypeStruct((rows, cols), F32),
            jax.ShapeDtypeStruct((rows, lanes), F32),
            jax.ShapeDtypeStruct((rows, lanes), BF16),
        ],
        in_specs=[VMEM] * (3 + len(grads)) + [pl.BlockSpec(memory_space=pl.ANY)] * len(after),
        out_specs=[VMEM] * 3,
        compiler_params=PARAMS,
    )(momentum, keep, table, *grads, *after)


def subtract_kernel(table_t_ref, *refs):
    new_ref = refs[-1]
    at = 0
    for blended_ref, coeff_ref in zip(refs[:-1:2], refs[1:-1:2]):
        for g in range(blended_ref.shape[1] // GROUP):
            new_ref[:, at : at + GROUP] = blended_ref[:, g * GROUP : (g + 1) * GROUP] - jnp.dot(
                coeff_ref[:, g * 128 : (g + 1) * 128],
                table_t_ref[...],
                precision=HIGHEST,
                preferred_element_type=F32,
            )
            at += GROUP


def subtract_rebuilt(table, parts, shape):
    return pl.pallas_call(
        subtract_kernel,
        out_shape=jax.ShapeDtypeStruct(shape, F32),
        in_specs=[VMEM] * (1 + len(parts)),
        out_specs=VMEM,
        compiler_params=PARAMS,
    )(table.T, *parts)


def combine_kernel(count, *refs):
    total_ref = refs[-1]
    at = 0
    for i in range(0, 4 * count, 4):
        own, one, two, three = (ref[...].astype(F32) for ref in refs[i : i + 4])
        total_ref[:, at : at + own.shape[1]] = (own + one) + (two + three)
        at += own.shape[1]


def combine(parts, after):
    count = len(parts) // 4
    rows = parts[0].shape[0]
    lanes = sum(part.shape[1] for part in parts[::4])
    return pl.pallas_call(
        functools.partial(combine_kernel, count),
        out_shape=jax.ShapeDtypeStruct((rows, lanes), F32),
        in_specs=[VMEM] * len(parts) + [pl.BlockSpec(memory_space=pl.ANY)] * len(after),
        out_specs=VMEM,
        compiler_params=PARAMS,
    )(*parts, *after)


def decode_kernel(mine_ref, other_ref, table_t_ref, update_ref):
    for g in range(update_ref.shape[1] // GROUP):
        lanes = slice(g * 128, (g + 1) * 128)
        coeffs = mine_ref[:, lanes] + other_ref[:, lanes]
        update_ref[:, g * GROUP : (g + 1) * GROUP] = jnp.dot(
            coeffs, table_t_ref[...], precision=HIGHEST, preferred_element_type=F32
        )


def decode(mine, other, table, width):
    return pl.pallas_call(
        decode_kernel,
        out_shape=jax.ShapeDtypeStruct((mine.shape[0], width), F32),
        in_specs=[VMEM] * 3,
        out_specs=VMEM,
        compiler_params=PARAMS,
    )(mine, other, table.T)


def swap(array, axis, d):
    return lax.ppermute(array, axis, [(i, i ^ d) for i in range(lax.axis_size(axis))])


def sides(nz):
    return [(c, z, 1 if (z + c) % 2 else -1) for c in range(2) for z in range(nz)]


def move(array, steps):
    nz = lax.axis_size("z")
    return lax.ppermute(array, ("core", "z"), [(c * nz + z, c * nz + (z + steps * side) % nz) for c, z, side in sides(nz)])


def reduce_over_z(kept, given, after):
    near, far = relay(kept, move(given, -1), after)
    far = move(far, 2)
    last = move((near[1] + far[1].astype(F32)).astype(BF16), 1)
    return [near, far, last]


def per_device(tokens, cotangent, weight, momentum, lengths, kept_index):
    ny, nz = lax.axis_size("y"), lax.axis_size("z")
    y = lax.axis_index("y").astype(jnp.int32).reshape(1)
    z = lax.axis_index("z").astype(jnp.int32)
    place = jnp.stack([z, 2 * ((z + lax.axis_index("core").astype(jnp.int32)) % 2) - 1])
    width = weight.shape[1]

    weight_quarter = lax.all_gather(weight, "z", axis=0, tiled=True)
    sent_two, sent_one, sent_three = split_inputs(y, lengths, tokens, cotangent, ny, (2, 1, 3))
    two = swap(sent_two, "y", 2)
    one, three = swap(sent_one, "y", 1), swap(sent_three, "y", 3)

    total, back_two = project_first(y, tokens, two, weight_quarter, ny)
    first = grad_first(y, lengths, tokens, cotangent, two, ny, weight_quarter)
    keep = keep_mask(kept_index)
    terms = grad_terms(place, first, one, three, nz, HALVES, (back_two, keep))
    back_one, back_three = project_rest(one, three, weight_quarter)
    backs = [swap(back_two, "y", 2), swap(back_one, "y", 1), swap(back_three, "y", 3)]

    table = group_table()
    sums, blends = [], []
    for h in range(HALVES):
        grads = reduce_over_z(*terms[2 * h : 2 * h + 2], (back_one, back_three, *backs[: 1 - h]))
        after = backs[1:] if h == HALVES - 1 else ()
        blended, coeffs, sent = encode(h * width // HALVES, momentum[0], keep, table, grads, after)
        blends += [blended, coeffs]
        sums += [sent] + [swap(sent, "x", d) for d in (1, 2, 3)]

    projected = (total + sum(back.astype(F32) for back in backs)).astype(BF16)
    new_momentum = subtract_rebuilt(table, blends, momentum.shape[1:])
    mine = combine(sums, (projected, new_momentum))
    update = decode(mine, swap(mine, "core", 1), table, width)
    return (projected, new_momentum[None], update)


def solution(mesh):
    fine = Mesh(mesh.devices.reshape(4, 2, 4, 8), ("x", "core", "y", "z"))
    rep, fsdp = ("x", "core"), ("y", "z")
    placed = (
        P(rep + fsdp, None),
        P(rep + fsdp, None),
        P(fsdp, None),
        P(rep, fsdp, None),
        P(rep + fsdp),
        P(fsdp, None),
    )
    return jax.shard_map(
        per_device,
        mesh=fine,
        in_specs=placed,
        out_specs=(P(rep + fsdp, None), P(rep, fsdp, None), P(fsdp, None)),
        check_vma=False,
    )
```

```python
import functools

import jax
import jax.numpy as jnp
import numpy as np
from jax import lax
from jax.experimental import pallas as pl
from jax.experimental.pallas import tpu as pltpu
from jax.sharding import Mesh, PartitionSpec as P

PIECE = 64
TOPK = 16
FREQ = 32
SLOT = 256
GROUP = 128 // FREQ * PIECE

HALVES = 2

BF16 = jnp.bfloat16
F32 = jnp.float32
HIGHEST = lax.Precision.HIGHEST
TOKEN = jax.ShapeDtypeStruct((8, 128), F32)
VMEM = pl.BlockSpec(memory_space=pltpu.VMEM)
SMEM = pl.BlockSpec(memory_space=pltpu.SMEM)
HBM = pl.BlockSpec(memory_space=pltpu.HBM)
PARAMS = pltpu.CompilerParams(vmem_limit_bytes=14 * 1024 * 1024)
ALL = pltpu.CompilerParams(vmem_limit_bytes=56 * 1024 * 1024)
BIG = pltpu.CompilerParams(vmem_limit_bytes=28 * 1024 * 1024)


def group_table():
    k = np.arange(FREQ)[:, None].astype(np.float64)
    n = np.arange(PIECE)[None, :].astype(np.float64)
    scale = np.where(k == 0, np.sqrt(1.0 / PIECE), np.sqrt(2.0 / PIECE))
    rows = scale * np.cos(np.pi * (2 * n + 1) * k / (2 * PIECE))
    return jnp.asarray(np.kron(np.eye(GROUP // PIECE), rows.T), F32)


def mask_rows(cot, length):
    position = lax.broadcasted_iota(jnp.int32, cot.shape, 0)
    return jnp.where(position < length, cot, jnp.zeros_like(cot))


def split_kernel(order, y_ref, length_ref, tok_ref, cot_ref, *refs):
    count = len(order)
    outs, bufs, (cot_buffer, in_sems, out_sems) = refs[:count], refs[count : 2 * count], refs[2 * count :]
    width = outs[0].shape[1] - cot_ref.shape[1]
    cot_copy = pltpu.make_async_copy(cot_ref, cot_buffer, in_sems.at[count])
    cot_copy.start()
    in_copies, out_copies = [], []
    for i, d in enumerate(order):
        start = pl.multiple_of(lax.bitwise_xor(y_ref[0], d) * width, width)
        copy = pltpu.make_async_copy(tok_ref.at[:, pl.ds(start, width)], bufs[i].at[:, :width], in_sems.at[i])
        copy.start()
        in_copies.append(copy)
        out_copies.append(pltpu.make_async_copy(bufs[i], outs[i], out_sems.at[i]))
    cot_copy.wait()
    masked = mask_rows(cot_buffer[...], length_ref[0])
    for buf, in_copy, out_copy in zip(bufs, in_copies, out_copies):
        buf[:, width:] = masked
        in_copy.wait()
        out_copy.start()
    for copy in out_copies:
        copy.wait()


def split_inputs(y, lengths, tokens, cotangent, ny, order):
    rows, width = tokens.shape[0], tokens.shape[1] // ny
    shape = (rows, width + cotangent.shape[1])
    count = len(order)
    return pl.pallas_call(
        functools.partial(split_kernel, order),
        out_shape=[jax.ShapeDtypeStruct(shape, BF16)] * count,
        in_specs=[SMEM, SMEM] + [HBM] * 2,
        out_specs=[pl.BlockSpec(memory_space=pl.ANY)] * count,
        scratch_shapes=[pltpu.VMEM(shape, BF16)] * count
        + [
            pltpu.VMEM(cotangent.shape, BF16),
            pltpu.SemaphoreType.DMA((count + 1,)),
            pltpu.SemaphoreType.DMA((count,)),
        ],
        compiler_params=ALL,
    )(y, lengths, tokens, cotangent)


def whole(array):
    return pl.BlockSpec(array.shape, lambda i, *scalars: (0,) * array.ndim)


def own_columns(tokens, ny):
    return pl.BlockSpec((tokens.shape[0], tokens.shape[1] // ny), lambda i, y, *scalars: (0, y[0]))


def contract_rows(left, right):
    return lax.dot_general(left, right, (((0,), (0,)), ((), ())), preferred_element_type=F32)


def grad_first_kernel(y_ref, length_ref, own_ref, cot_ref, both_ref, after_ref, acc_ref):
    width = own_ref.shape[1]
    acc_ref[...] = contract_rows(own_ref[...], mask_rows(cot_ref[...], length_ref[0]))
    acc_ref[...] = acc_ref[...] + contract_rows(both_ref[:, :width], both_ref[:, width:])


def grad_first(y, lengths, tokens, cotangent, both, ny, after):
    shape = (tokens.shape[1] // ny, cotangent.shape[1])
    return pl.pallas_call(
        grad_first_kernel,
        out_shape=jax.ShapeDtypeStruct(shape, F32),
        grid_spec=pltpu.PrefetchScalarGridSpec(
            num_scalar_prefetch=2,
            grid=(1,),
            in_specs=[
                own_columns(tokens, ny),
                whole(cotangent),
                whole(both),
                pl.BlockSpec(memory_space=pl.ANY),
            ],
            out_specs=pl.BlockSpec(shape, lambda i, *scalars: (0, 0)),
        ),
        compiler_params=BIG,
    )(y, lengths, tokens, cotangent, both, after)


def grad_kernel(nz, skip, place_ref, first_ref, one_ref, two_ref, *refs):
    outs, acc = refs[skip:-1], refs[-1]
    width = first_ref.shape[0]
    both = jnp.concatenate([one_ref[...], two_ref[...]], axis=0)
    acc[...] = first_ref[...] + contract_rows(both[:, :width], both[:, width:])

    rows = width // nz
    z, side = place_ref[0], place_ref[1]
    halves = len(outs) // 2
    cols = acc.shape[1] // halves

    def block(k, h):
        at = lax.rem(z + k * side + nz, nz)
        return acc[pl.ds(pl.multiple_of(at * rows, 16), rows), h * cols : (h + 1) * cols]

    for h in range(halves):
        kept, given = outs[2 * h : 2 * h + 2]
        for j in range(nz // 2):
            kept[j] = block(j, h)
            given[j] = block(-1 - j, h).astype(BF16)


def grad_terms(place, first, one, two, nz, halves, after):
    width, cols = first.shape
    shape = (nz // 2, width // nz, cols // halves)
    return pl.pallas_call(
        functools.partial(grad_kernel, nz, len(after)),
        out_shape=[jax.ShapeDtypeStruct(shape, F32), jax.ShapeDtypeStruct(shape, BF16)] * halves,
        in_specs=[SMEM] + [VMEM] * 3 + [pl.BlockSpec(memory_space=pl.ANY)] * len(after),
        out_specs=[VMEM] * (2 * halves),
        scratch_shapes=[pltpu.VMEM((width, cols), F32)],
        compiler_params=BIG,
    )(place, first, one, two, *after)


def relay_kernel(kept_ref, got_ref, *rest):
    near_ref, far_ref = rest[-2:]
    for j in range(2):
        near_ref[j] = kept_ref[j] + got_ref[j].astype(F32)
        far_ref[j] = (kept_ref[j + 2] + got_ref[j + 2].astype(F32)).astype(BF16)


def relay(kept, got, after):
    shape = (2, *kept.shape[1:])
    return pl.pallas_call(
        relay_kernel,
        out_shape=[jax.ShapeDtypeStruct(shape, F32), jax.ShapeDtypeStruct(shape, BF16)],
        in_specs=[VMEM] * 2 + [pl.BlockSpec(memory_space=pl.ANY)] * len(after),
        out_specs=[VMEM] * 2,
        compiler_params=PARAMS,
    )(kept, got, *after)


def project_first_kernel(y_ref, own_ref, both_ref, weight_ref, total_ref, out_ref):
    width = own_ref.shape[1]
    total_ref[...] = jnp.dot(own_ref[...], weight_ref[...], preferred_element_type=F32)
    out_ref[...] = jnp.dot(both_ref[:, :width], weight_ref[...], preferred_element_type=F32).astype(BF16)


def project_first(y, tokens, both, weight, ny):
    shape = (tokens.shape[0], weight.shape[1])
    return pl.pallas_call(
        project_first_kernel,
        out_shape=[jax.ShapeDtypeStruct(shape, F32), jax.ShapeDtypeStruct(shape, BF16)],
        grid_spec=pltpu.PrefetchScalarGridSpec(
            num_scalar_prefetch=1,
            grid=(1,),
            in_specs=[own_columns(tokens, ny), whole(both), whole(weight)],
            out_specs=[pl.BlockSpec(shape, lambda i, y: (0, 0))] * 2,
        ),
        compiler_params=BIG,
    )(y, tokens, both, weight)


def project_kernel(one_ref, two_ref, weight_ref, one_out, two_out):
    width = weight_ref.shape[0]
    for both, out in ((one_ref, one_out), (two_ref, two_out)):
        out[...] = jnp.dot(both[:, :width], weight_ref[...], preferred_element_type=F32).astype(BF16)


def project_rest(one, two, weight):
    shape = jax.ShapeDtypeStruct((one.shape[0], weight.shape[1]), BF16)
    return pl.pallas_call(
        project_kernel,
        out_shape=[shape, shape],
        in_specs=[VMEM] * 3,
        out_specs=[VMEM] * 2,
        compiler_params=PARAMS,
    )(one, two, weight)


def keep_kernel(kept_ref, keep_ref):
    kept = kept_ref[...].astype(F32).astype(BF16)
    rows, lanes = keep_ref.shape
    freq = lax.rem(lax.broadcasted_iota(jnp.int32, (rows, lanes), 1), FREQ).astype(F32)
    slot = lax.broadcasted_iota(jnp.int32, (kept.shape[1], lanes), 0)
    first = lax.broadcasted_iota(jnp.int32, (kept.shape[1], lanes), 1) // FREQ * TOPK
    keep = jnp.zeros((rows, lanes), F32)
    for j in range(TOPK):
        spread = (slot == first + j).astype(F32).astype(BF16)
        index = jnp.dot(kept, spread, preferred_element_type=F32)
        keep = jnp.where(index == freq, 1.0, keep)
    keep_ref[...] = keep


def keep_mask(kept_index):
    rows, slots = kept_index.shape
    return pl.pallas_call(
        keep_kernel,
        out_shape=jax.ShapeDtypeStruct((rows, slots // TOPK * FREQ), F32),
        in_specs=[VMEM],
        out_specs=VMEM,
        compiler_params=PARAMS,
    )(kept_index)


def encode_kernel(start, momentum_ref, keep_ref, table_ref, near_ref, far_ref, last_ref, *rest):
    blended_ref, coeff_ref, sent_ref = rest[-3:]
    for g in range(blended_ref.shape[1] // GROUP):
        cols = slice(g * GROUP, (g + 1) * GROUP)
        lanes = slice(g * 128, (g + 1) * 128)
        at = start + g * GROUP
        grad = near_ref[0, :, cols] + far_ref[0, :, cols].astype(F32) + last_ref[:, cols].astype(F32)
        blended = 0.9 * momentum_ref[:, at : at + GROUP] + grad
        coeffs = jnp.dot(blended, table_ref[...], precision=HIGHEST, preferred_element_type=F32)
        at = at // GROUP * 128
        coeffs = coeffs * keep_ref[:, at : at + 128]
        blended_ref[:, cols] = blended
        coeff_ref[:, lanes] = coeffs
        sent_ref[:, lanes] = coeffs.astype(BF16)


def encode(start, momentum, keep, table, grads, after):
    rows, cols = grads[2].shape
    lanes = cols // GROUP * 128
    return pl.pallas_call(
        functools.partial(encode_kernel, start),
        out_shape=[
            jax.ShapeDtypeStruct((rows, cols), F32),
            jax.ShapeDtypeStruct((rows, lanes), F32),
            jax.ShapeDtypeStruct((rows, lanes), BF16),
        ],
        in_specs=[VMEM] * (3 + len(grads)) + [pl.BlockSpec(memory_space=pl.ANY)] * len(after),
        out_specs=[VMEM] * 3,
        compiler_params=PARAMS,
    )(momentum, keep, table, *grads, *after)


def subtract_kernel(table_t_ref, *refs):
    parts, (new_ref, token_ref) = refs[:-2], refs[-2:]
    token_ref[...] = jnp.zeros_like(token_ref)
    at = 0
    for blended_ref, coeff_ref in zip(parts[::2], parts[1::2]):
        for g in range(blended_ref.shape[1] // GROUP):
            new_ref[:, at : at + GROUP] = blended_ref[:, g * GROUP : (g + 1) * GROUP] - jnp.dot(
                coeff_ref[:, g * 128 : (g + 1) * 128],
                table_t_ref[...],
                precision=HIGHEST,
                preferred_element_type=F32,
            )
            at += GROUP


def subtract_rebuilt(table, parts, shape):
    return pl.pallas_call(
        subtract_kernel,
        out_shape=[jax.ShapeDtypeStruct(shape, F32), TOKEN],
        in_specs=[VMEM] * (1 + len(parts)),
        out_specs=[VMEM] * 2,
        compiler_params=PARAMS,
    )(table.T, *parts)


def finish_kernel(total_ref, one_ref, two_ref, three_ref, out_ref, token_ref):
    token_ref[...] = jnp.zeros_like(token_ref)
    total = total_ref[...] + one_ref[...].astype(F32)
    out_ref[...] = (total + (two_ref[...].astype(F32) + three_ref[...].astype(F32))).astype(BF16)


def finish_projection(total, backs):
    return pl.pallas_call(
        finish_kernel,
        out_shape=[jax.ShapeDtypeStruct(total.shape, BF16), TOKEN],
        in_specs=[VMEM] * 4,
        out_specs=[VMEM] * 2,
        compiler_params=PARAMS,
    )(total, *backs)


def combine_kernel(count, *refs):
    total_ref = refs[-1]
    at = 0
    for i in range(0, 4 * count, 4):
        own, one, two, three = (ref[...].astype(F32) for ref in refs[i : i + 4])
        total_ref[:, at : at + own.shape[1]] = (own + one) + (two + three)
        at += own.shape[1]


def combine(parts, after):
    count = len(parts) // 4
    rows = parts[0].shape[0]
    lanes = sum(part.shape[1] for part in parts[::4])
    return pl.pallas_call(
        functools.partial(combine_kernel, count),
        out_shape=jax.ShapeDtypeStruct((rows, lanes), F32),
        in_specs=[VMEM] * len(parts) + [pl.BlockSpec(memory_space=pl.ANY)] * len(after),
        out_specs=VMEM,
        compiler_params=PARAMS,
    )(*parts, *after)


def decode_kernel(mine_ref, other_ref, table_t_ref, update_ref):
    for g in range(update_ref.shape[1] // GROUP):
        lanes = slice(g * 128, (g + 1) * 128)
        coeffs = mine_ref[:, lanes] + other_ref[:, lanes]
        update_ref[:, g * GROUP : (g + 1) * GROUP] = jnp.dot(
            coeffs, table_t_ref[...], precision=HIGHEST, preferred_element_type=F32
        )


def decode(mine, other, table, width):
    return pl.pallas_call(
        decode_kernel,
        out_shape=jax.ShapeDtypeStruct((mine.shape[0], width), F32),
        in_specs=[VMEM] * 3,
        out_specs=VMEM,
        compiler_params=PARAMS,
    )(mine, other, table.T)


def swap(array, axis, d):
    return lax.ppermute(array, axis, [(i, i ^ d) for i in range(lax.axis_size(axis))])


def sides(nz):
    return [(c, z, 1 if (z + c) % 2 else -1) for c in range(2) for z in range(nz)]


def move(array, steps):
    nz = lax.axis_size("z")
    return lax.ppermute(array, ("core", "z"), [(c * nz + z, c * nz + (z + steps * side) % nz) for c, z, side in sides(nz)])


def reduce_over_z(kept, given, after):
    near, far = relay(kept, move(given, -1), after)
    far = move(far, 2)
    last = move((near[1] + far[1].astype(F32)).astype(BF16), 1)
    return [near, far, last]


def per_device(tokens, cotangent, weight, momentum, lengths, kept_index):
    ny, nz = lax.axis_size("y"), lax.axis_size("z")
    y = lax.axis_index("y").astype(jnp.int32).reshape(1)
    z = lax.axis_index("z").astype(jnp.int32)
    place = jnp.stack([z, 2 * ((z + lax.axis_index("core").astype(jnp.int32)) % 2) - 1])
    width = weight.shape[1]

    weight_quarter = lax.all_gather(weight, "z", axis=0, tiled=True)
    (sent_two,) = split_inputs(y, lengths, tokens, cotangent, ny, (2,))
    sent_one, sent_three = split_inputs(y, lengths, tokens, cotangent, ny, (1, 3))
    two = swap(sent_two, "y", 2)
    one, three = swap(sent_one, "y", 1), swap(sent_three, "y", 3)

    total, back_two = project_first(y, tokens, two, weight_quarter, ny)
    first = grad_first(y, lengths, tokens, cotangent, two, ny, weight_quarter)
    keep = keep_mask(kept_index)
    terms = grad_terms(place, first, one, three, nz, HALVES, (back_two, keep))
    back_one, back_three = project_rest(one, three, weight_quarter)
    backs = [swap(back_two, "y", 2), swap(back_one, "y", 1), swap(back_three, "y", 3)]

    table = group_table()
    sums, blends = [], []
    for h in range(HALVES):
        last = h == HALVES - 1
        grads = reduce_over_z(*terms[2 * h : 2 * h + 2], (backs[0],) if last else (back_one, back_three))
        after = backs[1:] if last else ()
        blended, coeffs, sent = encode(h * width // HALVES, momentum[0], keep, table, grads, after)
        blends += [blended, coeffs]
        sums += [sent] + [swap(sent, "x", d) for d in (1, 2, 3)]

    projected, projected_token = finish_projection(total, backs)
    new_momentum, new_token = subtract_rebuilt(table, blends, momentum.shape[1:])
    mine = combine(sums, (projected_token, new_token))
    update = decode(mine, swap(mine, "core", 1), table, width)
    return (projected, new_momentum[None], update)


def solution(mesh):
    fine = Mesh(mesh.devices.reshape(4, 2, 4, 8), ("x", "core", "y", "z"))
    rep, fsdp = ("x", "core"), ("y", "z")
    placed = (
        P(rep + fsdp, None),
        P(rep + fsdp, None),
        P(fsdp, None),
        P(rep, fsdp, None),
        P(rep + fsdp),
        P(fsdp, None),
    )
    return jax.shard_map(
        per_device,
        mesh=fine,
        in_specs=placed,
        out_specs=(P(rep + fsdp, None), P(rep, fsdp, None), P(fsdp, None)),
        check_vma=False,
    )
```

```python
import functools

import jax
import jax.numpy as jnp
import numpy as np
from jax import lax
from jax.experimental import pallas as pl
from jax.experimental.pallas import tpu as pltpu
from jax.sharding import Mesh, PartitionSpec as P

PIECE = 64
TOPK = 16
FREQ = 32
SLOT = 256
GROUP = 128 // FREQ * PIECE

HALVES = 2

BF16 = jnp.bfloat16
F32 = jnp.float32
HIGHEST = lax.Precision.HIGHEST
TOKEN = jax.ShapeDtypeStruct((8, 128), F32)
VMEM = pl.BlockSpec(memory_space=pltpu.VMEM)
SMEM = pl.BlockSpec(memory_space=pltpu.SMEM)
HBM = pl.BlockSpec(memory_space=pltpu.HBM)
PARAMS = pltpu.CompilerParams(vmem_limit_bytes=14 * 1024 * 1024)
ALL = pltpu.CompilerParams(vmem_limit_bytes=56 * 1024 * 1024)
BIG = pltpu.CompilerParams(vmem_limit_bytes=28 * 1024 * 1024)


def group_table():
    k = np.arange(FREQ)[:, None].astype(np.float64)
    n = np.arange(PIECE)[None, :].astype(np.float64)
    scale = np.where(k == 0, np.sqrt(1.0 / PIECE), np.sqrt(2.0 / PIECE))
    rows = scale * np.cos(np.pi * (2 * n + 1) * k / (2 * PIECE))
    return jnp.asarray(np.kron(np.eye(GROUP // PIECE), rows.T), F32)


def mask_rows(cot, length):
    position = lax.broadcasted_iota(jnp.int32, cot.shape, 0)
    return jnp.where(position < length, cot, jnp.zeros_like(cot))


def split_kernel(order, y_ref, length_ref, tok_ref, cot_ref, *refs):
    count = len(order)
    outs, bufs, (cot_buffer, in_sems, out_sems) = refs[:count], refs[count : 2 * count], refs[2 * count :]
    width = outs[0].shape[1] - cot_ref.shape[1]
    cot_copy = pltpu.make_async_copy(cot_ref, cot_buffer, in_sems.at[count])
    cot_copy.start()
    in_copies, out_copies = [], []
    for i, d in enumerate(order):
        start = pl.multiple_of(lax.bitwise_xor(y_ref[0], d) * width, width)
        copy = pltpu.make_async_copy(tok_ref.at[:, pl.ds(start, width)], bufs[i].at[:, :width], in_sems.at[i])
        copy.start()
        in_copies.append(copy)
        out_copies.append(pltpu.make_async_copy(bufs[i], outs[i], out_sems.at[i]))
    cot_copy.wait()
    masked = mask_rows(cot_buffer[...], length_ref[0])
    for buf, in_copy, out_copy in zip(bufs, in_copies, out_copies):
        buf[:, width:] = masked
        in_copy.wait()
        out_copy.start()
    for copy in out_copies:
        copy.wait()


def split_inputs(y, lengths, tokens, cotangent, ny, order):
    rows, width = tokens.shape[0], tokens.shape[1] // ny
    shape = (rows, width + cotangent.shape[1])
    count = len(order)
    return pl.pallas_call(
        functools.partial(split_kernel, order),
        out_shape=[jax.ShapeDtypeStruct(shape, BF16)] * count,
        in_specs=[SMEM, SMEM] + [HBM] * 2,
        out_specs=[pl.BlockSpec(memory_space=pl.ANY)] * count,
        scratch_shapes=[pltpu.VMEM(shape, BF16)] * count
        + [
            pltpu.VMEM(cotangent.shape, BF16),
            pltpu.SemaphoreType.DMA((count + 1,)),
            pltpu.SemaphoreType.DMA((count,)),
        ],
        compiler_params=ALL,
    )(y, lengths, tokens, cotangent)


def whole(array):
    return pl.BlockSpec(array.shape, lambda i, *scalars: (0,) * array.ndim)


def own_columns(tokens, ny):
    return pl.BlockSpec((tokens.shape[0], tokens.shape[1] // ny), lambda i, y, *scalars: (0, y[0]))


def contract_rows(left, right):
    return lax.dot_general(left, right, (((0,), (0,)), ((), ())), preferred_element_type=F32)


def grad_first_kernel(y_ref, length_ref, own_ref, cot_ref, both_ref, after_ref, acc_ref):
    width = own_ref.shape[1]
    acc_ref[...] = contract_rows(own_ref[...], mask_rows(cot_ref[...], length_ref[0]))
    acc_ref[...] = acc_ref[...] + contract_rows(both_ref[:, :width], both_ref[:, width:])


def grad_first(y, lengths, tokens, cotangent, both, ny, after):
    shape = (tokens.shape[1] // ny, cotangent.shape[1])
    return pl.pallas_call(
        grad_first_kernel,
        out_shape=jax.ShapeDtypeStruct(shape, F32),
        grid_spec=pltpu.PrefetchScalarGridSpec(
            num_scalar_prefetch=2,
            grid=(1,),
            in_specs=[
                own_columns(tokens, ny),
                whole(cotangent),
                whole(both),
                pl.BlockSpec(memory_space=pl.ANY),
            ],
            out_specs=pl.BlockSpec(shape, lambda i, *scalars: (0, 0)),
        ),
        compiler_params=BIG,
    )(y, lengths, tokens, cotangent, both, after)


def grad_kernel(nz, skip, place_ref, first_ref, one_ref, two_ref, *refs):
    outs, acc = refs[skip:-1], refs[-1]
    width = first_ref.shape[0]
    both = jnp.concatenate([one_ref[...], two_ref[...]], axis=0)
    acc[...] = first_ref[...] + contract_rows(both[:, :width], both[:, width:])

    rows = width // nz
    z, side = place_ref[0], place_ref[1]
    halves = len(outs) // 2
    cols = acc.shape[1] // halves

    def block(k, h):
        at = lax.rem(z + k * side + nz, nz)
        return acc[pl.ds(pl.multiple_of(at * rows, 16), rows), h * cols : (h + 1) * cols]

    for h in range(halves):
        kept, given = outs[2 * h : 2 * h + 2]
        for j in range(nz // 2):
            kept[j] = block(j, h)
            given[j] = block(-1 - j, h).astype(BF16)


def grad_terms(place, first, one, two, nz, halves, after):
    width, cols = first.shape
    shape = (nz // 2, width // nz, cols // halves)
    return pl.pallas_call(
        functools.partial(grad_kernel, nz, len(after)),
        out_shape=[jax.ShapeDtypeStruct(shape, F32), jax.ShapeDtypeStruct(shape, BF16)] * halves,
        in_specs=[SMEM] + [VMEM] * 3 + [pl.BlockSpec(memory_space=pl.ANY)] * len(after),
        out_specs=[VMEM] * (2 * halves),
        scratch_shapes=[pltpu.VMEM((width, cols), F32)],
        compiler_params=BIG,
    )(place, first, one, two, *after)


def relay_kernel(kept_ref, got_ref, *rest):
    near_ref, far_ref = rest[-2:]
    for j in range(2):
        near_ref[j] = kept_ref[j] + got_ref[j].astype(F32)
        far_ref[j] = (kept_ref[j + 2] + got_ref[j + 2].astype(F32)).astype(BF16)


def relay(kept, got, after):
    shape = (2, *kept.shape[1:])
    return pl.pallas_call(
        relay_kernel,
        out_shape=[jax.ShapeDtypeStruct(shape, F32), jax.ShapeDtypeStruct(shape, BF16)],
        in_specs=[VMEM] * 2 + [pl.BlockSpec(memory_space=pl.ANY)] * len(after),
        out_specs=[VMEM] * 2,
        compiler_params=PARAMS,
    )(kept, got, *after)


def project_first_kernel(y_ref, own_ref, both_ref, weight_ref, total_ref, out_ref):
    width = own_ref.shape[1]
    total_ref[...] = jnp.dot(own_ref[...], weight_ref[...], preferred_element_type=F32)
    out_ref[...] = jnp.dot(both_ref[:, :width], weight_ref[...], preferred_element_type=F32).astype(BF16)


def project_first(y, tokens, both, weight, ny):
    shape = (tokens.shape[0], weight.shape[1])
    return pl.pallas_call(
        project_first_kernel,
        out_shape=[jax.ShapeDtypeStruct(shape, F32), jax.ShapeDtypeStruct(shape, BF16)],
        grid_spec=pltpu.PrefetchScalarGridSpec(
            num_scalar_prefetch=1,
            grid=(1,),
            in_specs=[own_columns(tokens, ny), whole(both), whole(weight)],
            out_specs=[pl.BlockSpec(shape, lambda i, y: (0, 0))] * 2,
        ),
        compiler_params=BIG,
    )(y, tokens, both, weight)


def project_kernel(one_ref, two_ref, weight_ref, one_out, two_out):
    width = weight_ref.shape[0]
    for both, out in ((one_ref, one_out), (two_ref, two_out)):
        out[...] = jnp.dot(both[:, :width], weight_ref[...], preferred_element_type=F32).astype(BF16)


def project_rest(one, two, weight):
    shape = jax.ShapeDtypeStruct((one.shape[0], weight.shape[1]), BF16)
    return pl.pallas_call(
        project_kernel,
        out_shape=[shape, shape],
        in_specs=[VMEM] * 3,
        out_specs=[VMEM] * 2,
        compiler_params=PARAMS,
    )(one, two, weight)


def keep_kernel(kept_ref, keep_ref):
    kept = kept_ref[...].astype(F32).astype(BF16)
    rows, lanes = keep_ref.shape
    freq = lax.rem(lax.broadcasted_iota(jnp.int32, (rows, lanes), 1), FREQ).astype(F32)
    slot = lax.broadcasted_iota(jnp.int32, (kept.shape[1], lanes), 0)
    first = lax.broadcasted_iota(jnp.int32, (kept.shape[1], lanes), 1) // FREQ * TOPK
    keep = jnp.zeros((rows, lanes), F32)
    for j in range(TOPK):
        spread = (slot == first + j).astype(F32).astype(BF16)
        index = jnp.dot(kept, spread, preferred_element_type=F32)
        keep = jnp.where(index == freq, 1.0, keep)
    keep_ref[...] = keep


def keep_mask(kept_index):
    rows, slots = kept_index.shape
    return pl.pallas_call(
        keep_kernel,
        out_shape=jax.ShapeDtypeStruct((rows, slots // TOPK * FREQ), F32),
        in_specs=[VMEM],
        out_specs=VMEM,
        compiler_params=PARAMS,
    )(kept_index)


def encode_kernel(start, momentum_ref, keep_ref, table_ref, near_ref, far_ref, last_ref, *rest):
    blended_ref, coeff_ref, sent_ref = rest[-3:]
    for g in range(blended_ref.shape[1] // GROUP):
        cols = slice(g * GROUP, (g + 1) * GROUP)
        lanes = slice(g * 128, (g + 1) * 128)
        at = start + g * GROUP
        grad = near_ref[0, :, cols] + far_ref[0, :, cols].astype(F32) + last_ref[:, cols].astype(F32)
        blended = 0.9 * momentum_ref[:, at : at + GROUP] + grad
        coeffs = jnp.dot(blended, table_ref[...], precision=HIGHEST, preferred_element_type=F32)
        at = at // GROUP * 128
        coeffs = coeffs * keep_ref[:, at : at + 128]
        blended_ref[:, cols] = blended
        coeff_ref[:, lanes] = coeffs
        sent_ref[:, lanes] = coeffs.astype(BF16)


def encode(start, momentum, keep, table, grads, after):
    rows, cols = grads[2].shape
    lanes = cols // GROUP * 128
    return pl.pallas_call(
        functools.partial(encode_kernel, start),
        out_shape=[
            jax.ShapeDtypeStruct((rows, cols), F32),
            jax.ShapeDtypeStruct((rows, lanes), F32),
            jax.ShapeDtypeStruct((rows, lanes), BF16),
        ],
        in_specs=[VMEM] * (3 + len(grads)) + [pl.BlockSpec(memory_space=pl.ANY)] * len(after),
        out_specs=[VMEM] * 3,
        compiler_params=PARAMS,
    )(momentum, keep, table, *grads, *after)


def subtract_kernel(table_t_ref, *refs):
    parts, (new_ref, token_ref) = refs[:-2], refs[-2:]
    token_ref[...] = jnp.zeros_like(token_ref)
    at = 0
    for blended_ref, coeff_ref in zip(parts[::2], parts[1::2]):
        for g in range(blended_ref.shape[1] // GROUP):
            new_ref[:, at : at + GROUP] = blended_ref[:, g * GROUP : (g + 1) * GROUP] - jnp.dot(
                coeff_ref[:, g * 128 : (g + 1) * 128],
                table_t_ref[...],
                precision=HIGHEST,
                preferred_element_type=F32,
            )
            at += GROUP


def subtract_rebuilt(table, parts, shape):
    return pl.pallas_call(
        subtract_kernel,
        out_shape=[jax.ShapeDtypeStruct(shape, F32), TOKEN],
        in_specs=[VMEM] * (1 + len(parts)),
        out_specs=[VMEM] * 2,
        compiler_params=PARAMS,
    )(table.T, *parts)


def finish_kernel(total_ref, one_ref, two_ref, three_ref, out_ref, token_ref):
    token_ref[...] = jnp.zeros_like(token_ref)
    total = total_ref[...] + one_ref[...].astype(F32)
    out_ref[...] = (total + (two_ref[...].astype(F32) + three_ref[...].astype(F32))).astype(BF16)


def finish_projection(total, backs):
    return pl.pallas_call(
        finish_kernel,
        out_shape=[jax.ShapeDtypeStruct(total.shape, BF16), TOKEN],
        in_specs=[VMEM] * 4,
        out_specs=[VMEM] * 2,
        compiler_params=PARAMS,
    )(total, *backs)


def combine_kernel(count, *refs):
    total_ref = refs[-1]
    at = 0
    for i in range(0, 4 * count, 4):
        own, one, two, three = (ref[...].astype(F32) for ref in refs[i : i + 4])
        total_ref[:, at : at + own.shape[1]] = (own + one) + (two + three)
        at += own.shape[1]


def combine(parts, after):
    count = len(parts) // 4
    rows = parts[0].shape[0]
    lanes = sum(part.shape[1] for part in parts[::4])
    return pl.pallas_call(
        functools.partial(combine_kernel, count),
        out_shape=jax.ShapeDtypeStruct((rows, lanes), F32),
        in_specs=[VMEM] * len(parts) + [pl.BlockSpec(memory_space=pl.ANY)] * len(after),
        out_specs=VMEM,
        compiler_params=PARAMS,
    )(*parts, *after)


def decode_kernel(mine_ref, other_ref, table_t_ref, *rest):
    update_ref = rest[-1]
    for g in range(update_ref.shape[1] // GROUP):
        lanes = slice(g * 128, (g + 1) * 128)
        coeffs = mine_ref[:, lanes] + other_ref[:, lanes]
        update_ref[:, g * GROUP : (g + 1) * GROUP] = jnp.dot(
            coeffs, table_t_ref[...], precision=HIGHEST, preferred_element_type=F32
        )


def decode(h, mine, other, table, width, made):
    rows, lanes = mine.shape
    cols = lanes // 128 * GROUP
    whole_block = lambda array: pl.BlockSpec(array.shape, lambda i: (0, 0))
    operands = (mine, other, table.T)
    return pl.pallas_call(
        decode_kernel,
        grid=(1,),
        out_shape=jax.ShapeDtypeStruct((rows, width), F32),
        in_specs=[whole_block(array) for array in operands] + [pl.BlockSpec(memory_space=pl.ANY)] * len(made),
        out_specs=pl.BlockSpec((rows, cols), lambda i: (0, h)),
        input_output_aliases={len(operands): 0} if made else {},
        compiler_params=PARAMS,
    )(*operands, *made)


def swap(array, axis, d):
    return lax.ppermute(array, axis, [(i, i ^ d) for i in range(lax.axis_size(axis))])


def sides(nz):
    return [(c, z, 1 if (z + c) % 2 else -1) for c in range(2) for z in range(nz)]


def move(array, steps):
    nz = lax.axis_size("z")
    return lax.ppermute(array, ("core", "z"), [(c * nz + z, c * nz + (z + steps * side) % nz) for c, z, side in sides(nz)])


def reduce_over_z(kept, given, after):
    near, far = relay(kept, move(given, -1), after)
    far = move(far, 2)
    last = move((near[1] + far[1].astype(F32)).astype(BF16), 1)
    return [near, far, last]


def per_device(tokens, cotangent, weight, momentum, lengths, kept_index):
    ny, nz = lax.axis_size("y"), lax.axis_size("z")
    y = lax.axis_index("y").astype(jnp.int32).reshape(1)
    z = lax.axis_index("z").astype(jnp.int32)
    place = jnp.stack([z, 2 * ((z + lax.axis_index("core").astype(jnp.int32)) % 2) - 1])
    width = weight.shape[1]

    weight_quarter = lax.all_gather(weight, "z", axis=0, tiled=True)
    (sent_two,) = split_inputs(y, lengths, tokens, cotangent, ny, (2,))
    sent_one, sent_three = split_inputs(y, lengths, tokens, cotangent, ny, (1, 3))
    two = swap(sent_two, "y", 2)
    one, three = swap(sent_one, "y", 1), swap(sent_three, "y", 3)

    total, back_two = project_first(y, tokens, two, weight_quarter, ny)
    first = grad_first(y, lengths, tokens, cotangent, two, ny, weight_quarter)
    keep = keep_mask(kept_index)
    terms = grad_terms(place, first, one, three, nz, HALVES, (back_two, keep))
    back_one, back_three = project_rest(one, three, weight_quarter)
    backs = [swap(back_two, "y", 2), swap(back_one, "y", 1), swap(back_three, "y", 3)]

    table = group_table()
    sums, blends = [], []
    for h in range(HALVES):
        last = h == HALVES - 1
        grads = reduce_over_z(*terms[2 * h : 2 * h + 2], (backs[0],) if last else (back_one, back_three))
        after = backs[1:] if last else ()
        blended, coeffs, sent = encode(h * width // HALVES, momentum[0], keep, table, grads, after)
        blends += [blended, coeffs]
        sums += [sent] + [swap(sent, "x", d) for d in (1, 2, 3)]

    projected, projected_token = finish_projection(total, backs)
    new_momentum, new_token = subtract_rebuilt(table, blends, momentum.shape[1:])
    made = ()
    for h in range(HALVES):
        after = (projected_token, new_token) if h == HALVES - 1 else ()
        mine = combine(sums[4 * h : 4 * h + 4], after)
        made = (decode(h, mine, swap(mine, "core", 1), table, width, made),)
    (update,) = made
    return (projected, new_momentum[None], update)


def solution(mesh):
    fine = Mesh(mesh.devices.reshape(4, 2, 4, 8), ("x", "core", "y", "z"))
    rep, fsdp = ("x", "core"), ("y", "z")
    placed = (
        P(rep + fsdp, None),
        P(rep + fsdp, None),
        P(fsdp, None),
        P(rep, fsdp, None),
        P(rep + fsdp),
        P(fsdp, None),
    )
    return jax.shard_map(
        per_device,
        mesh=fine,
        in_specs=placed,
        out_specs=(P(rep + fsdp, None), P(rep, fsdp, None), P(fsdp, None)),
        check_vma=False,
    )
```

```python
import functools

import jax
import jax.numpy as jnp
import numpy as np
from jax import lax
from jax.experimental import pallas as pl
from jax.experimental.pallas import tpu as pltpu
from jax.sharding import Mesh, PartitionSpec as P

PIECE = 64
TOPK = 16
FREQ = 32
SLOT = 256
GROUP = 128 // FREQ * PIECE

HALVES = 2

BF16 = jnp.bfloat16
F32 = jnp.float32
HIGHEST = lax.Precision.HIGHEST
TOKEN = jax.ShapeDtypeStruct((8, 128), F32)
VMEM = pl.BlockSpec(memory_space=pltpu.VMEM)
SMEM = pl.BlockSpec(memory_space=pltpu.SMEM)
HBM = pl.BlockSpec(memory_space=pltpu.HBM)
PARAMS = pltpu.CompilerParams(vmem_limit_bytes=14 * 1024 * 1024)
ALL = pltpu.CompilerParams(vmem_limit_bytes=56 * 1024 * 1024)
BIG = pltpu.CompilerParams(vmem_limit_bytes=28 * 1024 * 1024)


def group_table():
    k = np.arange(FREQ)[:, None].astype(np.float64)
    n = np.arange(PIECE)[None, :].astype(np.float64)
    scale = np.where(k == 0, np.sqrt(1.0 / PIECE), np.sqrt(2.0 / PIECE))
    rows = scale * np.cos(np.pi * (2 * n + 1) * k / (2 * PIECE))
    return jnp.asarray(np.kron(np.eye(GROUP // PIECE), rows.T), F32)


def mask_rows(cot, length):
    position = lax.broadcasted_iota(jnp.int32, cot.shape, 0)
    return jnp.where(position < length, cot, jnp.zeros_like(cot))


def split_kernel(order, y_ref, length_ref, tok_ref, cot_ref, *refs):
    count = len(order)
    outs, bufs, (cot_buffer, in_sems, out_sems) = refs[:count], refs[count : 2 * count], refs[2 * count :]
    width = outs[0].shape[1] - cot_ref.shape[1]
    cot_copy = pltpu.make_async_copy(cot_ref, cot_buffer, in_sems.at[count])
    cot_copy.start()
    in_copies, out_copies = [], []
    for i, d in enumerate(order):
        start = pl.multiple_of(lax.bitwise_xor(y_ref[0], d) * width, width)
        copy = pltpu.make_async_copy(tok_ref.at[:, pl.ds(start, width)], bufs[i].at[:, :width], in_sems.at[i])
        copy.start()
        in_copies.append(copy)
        for j, part in enumerate((pl.ds(0, width), pl.ds(width, cot_ref.shape[1]))):
            copy = pltpu.make_async_copy(bufs[i].at[:, part], outs[i].at[:, part], out_sems.at[2 * i + j])
            out_copies.append(copy)
    cot_copy.wait()
    masked = mask_rows(cot_buffer[...], length_ref[0])
    for i, buf in enumerate(bufs):
        buf[:, width:] = masked
        out_copies[2 * i + 1].start()
        in_copies[i].wait()
        out_copies[2 * i].start()
    for copy in out_copies:
        copy.wait()


def split_inputs(y, lengths, tokens, cotangent, ny, order):
    rows, width = tokens.shape[0], tokens.shape[1] // ny
    shape = (rows, width + cotangent.shape[1])
    count = len(order)
    return pl.pallas_call(
        functools.partial(split_kernel, order),
        out_shape=[jax.ShapeDtypeStruct(shape, BF16)] * count,
        in_specs=[SMEM, SMEM] + [HBM] * 2,
        out_specs=[pl.BlockSpec(memory_space=pl.ANY)] * count,
        scratch_shapes=[pltpu.VMEM(shape, BF16)] * count
        + [
            pltpu.VMEM(cotangent.shape, BF16),
            pltpu.SemaphoreType.DMA((count + 1,)),
            pltpu.SemaphoreType.DMA((2 * count,)),
        ],
        compiler_params=ALL,
    )(y, lengths, tokens, cotangent)


def whole(array):
    return pl.BlockSpec(array.shape, lambda i, *scalars: (0,) * array.ndim)


def own_columns(tokens, ny):
    return pl.BlockSpec((tokens.shape[0], tokens.shape[1] // ny), lambda i, y, *scalars: (0, y[0]))


def contract_rows(left, right):
    return lax.dot_general(left, right, (((0,), (0,)), ((), ())), preferred_element_type=F32)


def grad_first_kernel(y_ref, length_ref, own_ref, cot_ref, both_ref, after_ref, acc_ref):
    width = own_ref.shape[1]
    acc_ref[...] = contract_rows(own_ref[...], mask_rows(cot_ref[...], length_ref[0]))
    acc_ref[...] = acc_ref[...] + contract_rows(both_ref[:, :width], both_ref[:, width:])


def grad_first(y, lengths, tokens, cotangent, both, ny, after):
    shape = (tokens.shape[1] // ny, cotangent.shape[1])
    return pl.pallas_call(
        grad_first_kernel,
        out_shape=jax.ShapeDtypeStruct(shape, F32),
        grid_spec=pltpu.PrefetchScalarGridSpec(
            num_scalar_prefetch=2,
            grid=(1,),
            in_specs=[
                own_columns(tokens, ny),
                whole(cotangent),
                whole(both),
                pl.BlockSpec(memory_space=pl.ANY),
            ],
            out_specs=pl.BlockSpec(shape, lambda i, *scalars: (0, 0)),
        ),
        compiler_params=BIG,
    )(y, lengths, tokens, cotangent, both, after)


def grad_kernel(nz, skip, place_ref, first_ref, one_ref, two_ref, *refs):
    outs, acc = refs[skip:-1], refs[-1]
    width = first_ref.shape[0]
    both = jnp.concatenate([one_ref[...], two_ref[...]], axis=0)
    acc[...] = first_ref[...] + contract_rows(both[:, :width], both[:, width:])

    rows = width // nz
    z, side = place_ref[0], place_ref[1]
    halves = len(outs) // 2
    cols = acc.shape[1] // halves

    def block(k, h):
        at = lax.rem(z + k * side + nz, nz)
        return acc[pl.ds(pl.multiple_of(at * rows, 16), rows), h * cols : (h + 1) * cols]

    for h in range(halves):
        kept, given = outs[2 * h : 2 * h + 2]
        for j in range(nz // 2):
            kept[j] = block(j, h)
            given[j] = block(-1 - j, h).astype(BF16)


def grad_terms(place, first, one, two, nz, halves, after):
    width, cols = first.shape
    shape = (nz // 2, width // nz, cols // halves)
    return pl.pallas_call(
        functools.partial(grad_kernel, nz, len(after)),
        out_shape=[jax.ShapeDtypeStruct(shape, F32), jax.ShapeDtypeStruct(shape, BF16)] * halves,
        in_specs=[SMEM] + [VMEM] * 3 + [pl.BlockSpec(memory_space=pl.ANY)] * len(after),
        out_specs=[VMEM] * (2 * halves),
        scratch_shapes=[pltpu.VMEM((width, cols), F32)],
        compiler_params=BIG,
    )(place, first, one, two, *after)


def relay_kernel(kept_ref, got_ref, *rest):
    near_ref, far_ref = rest[-2:]
    for j in range(2):
        near_ref[j] = kept_ref[j] + got_ref[j].astype(F32)
        far_ref[j] = (kept_ref[j + 2] + got_ref[j + 2].astype(F32)).astype(BF16)


def relay(kept, got, after):
    shape = (2, *kept.shape[1:])
    return pl.pallas_call(
        relay_kernel,
        out_shape=[jax.ShapeDtypeStruct(shape, F32), jax.ShapeDtypeStruct(shape, BF16)],
        in_specs=[VMEM] * 2 + [pl.BlockSpec(memory_space=pl.ANY)] * len(after),
        out_specs=[VMEM] * 2,
        compiler_params=PARAMS,
    )(kept, got, *after)


def project_first_kernel(y_ref, own_ref, both_ref, weight_ref, total_ref, out_ref):
    width = own_ref.shape[1]
    total_ref[...] = jnp.dot(own_ref[...], weight_ref[...], preferred_element_type=F32)
    out_ref[...] = jnp.dot(both_ref[:, :width], weight_ref[...], preferred_element_type=F32).astype(BF16)


def project_first(y, tokens, both, weight, ny):
    shape = (tokens.shape[0], weight.shape[1])
    return pl.pallas_call(
        project_first_kernel,
        out_shape=[jax.ShapeDtypeStruct(shape, F32), jax.ShapeDtypeStruct(shape, BF16)],
        grid_spec=pltpu.PrefetchScalarGridSpec(
            num_scalar_prefetch=1,
            grid=(1,),
            in_specs=[own_columns(tokens, ny), whole(both), whole(weight)],
            out_specs=[pl.BlockSpec(shape, lambda i, y: (0, 0))] * 2,
        ),
        compiler_params=BIG,
    )(y, tokens, both, weight)


def project_kernel(one_ref, two_ref, weight_ref, one_out, two_out):
    width = weight_ref.shape[0]
    for both, out in ((one_ref, one_out), (two_ref, two_out)):
        out[...] = jnp.dot(both[:, :width], weight_ref[...], preferred_element_type=F32).astype(BF16)


def project_rest(one, two, weight):
    shape = jax.ShapeDtypeStruct((one.shape[0], weight.shape[1]), BF16)
    return pl.pallas_call(
        project_kernel,
        out_shape=[shape, shape],
        in_specs=[VMEM] * 3,
        out_specs=[VMEM] * 2,
        compiler_params=PARAMS,
    )(one, two, weight)


def keep_kernel(kept_ref, keep_ref):
    kept = kept_ref[...].astype(F32).astype(BF16)
    rows, lanes = keep_ref.shape
    freq = lax.rem(lax.broadcasted_iota(jnp.int32, (rows, lanes), 1), FREQ).astype(F32)
    slot = lax.broadcasted_iota(jnp.int32, (kept.shape[1], lanes), 0)
    first = lax.broadcasted_iota(jnp.int32, (kept.shape[1], lanes), 1) // FREQ * TOPK
    keep = jnp.zeros((rows, lanes), F32)
    for j in range(TOPK):
        spread = (slot == first + j).astype(F32).astype(BF16)
        index = jnp.dot(kept, spread, preferred_element_type=F32)
        keep = jnp.where(index == freq, 1.0, keep)
    keep_ref[...] = keep


def keep_mask(kept_index):
    rows, slots = kept_index.shape
    return pl.pallas_call(
        keep_kernel,
        out_shape=jax.ShapeDtypeStruct((rows, slots // TOPK * FREQ), F32),
        in_specs=[VMEM],
        out_specs=VMEM,
        compiler_params=PARAMS,
    )(kept_index)


def encode_kernel(start, momentum_ref, keep_ref, table_ref, near_ref, far_ref, last_ref, *rest):
    blended_ref, coeff_ref, sent_ref = rest[-3:]
    for g in range(blended_ref.shape[1] // GROUP):
        cols = slice(g * GROUP, (g + 1) * GROUP)
        lanes = slice(g * 128, (g + 1) * 128)
        at = start + g * GROUP
        grad = near_ref[0, :, cols] + far_ref[0, :, cols].astype(F32) + last_ref[:, cols].astype(F32)
        blended = 0.9 * momentum_ref[:, at : at + GROUP] + grad
        coeffs = jnp.dot(blended, table_ref[...], precision=HIGHEST, preferred_element_type=F32)
        at = at // GROUP * 128
        coeffs = coeffs * keep_ref[:, at : at + 128]
        blended_ref[:, cols] = blended
        coeff_ref[:, lanes] = coeffs
        sent_ref[:, lanes] = coeffs.astype(BF16)


def encode(start, momentum, keep, table, grads, after):
    rows, cols = grads[2].shape
    lanes = cols // GROUP * 128
    return pl.pallas_call(
        functools.partial(encode_kernel, start),
        out_shape=[
            jax.ShapeDtypeStruct((rows, cols), F32),
            jax.ShapeDtypeStruct((rows, lanes), F32),
            jax.ShapeDtypeStruct((rows, lanes), BF16),
        ],
        in_specs=[VMEM] * (3 + len(grads)) + [pl.BlockSpec(memory_space=pl.ANY)] * len(after),
        out_specs=[VMEM] * 3,
        compiler_params=PARAMS,
    )(momentum, keep, table, *grads, *after)


def subtract_kernel(table_t_ref, *refs):
    parts, (new_ref, token_ref) = refs[:-2], refs[-2:]
    token_ref[...] = jnp.zeros_like(token_ref)
    at = 0
    for blended_ref, coeff_ref in zip(parts[::2], parts[1::2]):
        for g in range(blended_ref.shape[1] // GROUP):
            new_ref[:, at : at + GROUP] = blended_ref[:, g * GROUP : (g + 1) * GROUP] - jnp.dot(
                coeff_ref[:, g * 128 : (g + 1) * 128],
                table_t_ref[...],
                precision=HIGHEST,
                preferred_element_type=F32,
            )
            at += GROUP


def subtract_rebuilt(table, parts, shape):
    return pl.pallas_call(
        subtract_kernel,
        out_shape=[jax.ShapeDtypeStruct(shape, F32), TOKEN],
        in_specs=[VMEM] * (1 + len(parts)),
        out_specs=[VMEM] * 2,
        compiler_params=PARAMS,
    )(table.T, *parts)


def finish_kernel(total_ref, one_ref, two_ref, three_ref, out_ref, token_ref):
    token_ref[...] = jnp.zeros_like(token_ref)
    total = total_ref[...] + one_ref[...].astype(F32)
    out_ref[...] = (total + (two_ref[...].astype(F32) + three_ref[...].astype(F32))).astype(BF16)


def finish_projection(total, backs):
    return pl.pallas_call(
        finish_kernel,
        out_shape=[jax.ShapeDtypeStruct(total.shape, BF16), TOKEN],
        in_specs=[VMEM] * 4,
        out_specs=[VMEM] * 2,
        compiler_params=PARAMS,
    )(total, *backs)


def combine_kernel(count, *refs):
    total_ref = refs[-1]
    at = 0
    for i in range(0, 4 * count, 4):
        own, one, two, three = (ref[...].astype(F32) for ref in refs[i : i + 4])
        total_ref[:, at : at + own.shape[1]] = (own + one) + (two + three)
        at += own.shape[1]


def combine(parts, after):
    count = len(parts) // 4
    rows = parts[0].shape[0]
    lanes = sum(part.shape[1] for part in parts[::4])
    return pl.pallas_call(
        functools.partial(combine_kernel, count),
        out_shape=jax.ShapeDtypeStruct((rows, lanes), F32),
        in_specs=[VMEM] * len(parts) + [pl.BlockSpec(memory_space=pl.ANY)] * len(after),
        out_specs=VMEM,
        compiler_params=PARAMS,
    )(*parts, *after)


def decode_kernel(mine_ref, other_ref, table_t_ref, *rest):
    update_ref = rest[-1]
    for g in range(update_ref.shape[1] // GROUP):
        lanes = slice(g * 128, (g + 1) * 128)
        coeffs = mine_ref[:, lanes] + other_ref[:, lanes]
        update_ref[:, g * GROUP : (g + 1) * GROUP] = jnp.dot(
            coeffs, table_t_ref[...], precision=HIGHEST, preferred_element_type=F32
        )


def decode(h, mine, other, table, width, made):
    rows, lanes = mine.shape
    cols = lanes // 128 * GROUP
    whole_block = lambda array: pl.BlockSpec(array.shape, lambda i: (0, 0))
    operands = (mine, other, table.T)
    return pl.pallas_call(
        decode_kernel,
        grid=(1,),
        out_shape=jax.ShapeDtypeStruct((rows, width), F32),
        in_specs=[whole_block(array) for array in operands] + [pl.BlockSpec(memory_space=pl.ANY)] * len(made),
        out_specs=pl.BlockSpec((rows, cols), lambda i: (0, h)),
        input_output_aliases={len(operands): 0} if made else {},
        compiler_params=PARAMS,
    )(*operands, *made)


def swap(array, axis, d):
    return lax.ppermute(array, axis, [(i, i ^ d) for i in range(lax.axis_size(axis))])


def sides(nz):
    return [(c, z, 1 if (z + c) % 2 else -1) for c in range(2) for z in range(nz)]


def move(array, steps):
    nz = lax.axis_size("z")
    return lax.ppermute(array, ("core", "z"), [(c * nz + z, c * nz + (z + steps * side) % nz) for c, z, side in sides(nz)])


def reduce_over_z(kept, given, after):
    near, far = relay(kept, move(given, -1), after)
    far = move(far, 2)
    last = move((near[1] + far[1].astype(F32)).astype(BF16), 1)
    return [near, far, last]


def per_device(tokens, cotangent, weight, momentum, lengths, kept_index):
    ny, nz = lax.axis_size("y"), lax.axis_size("z")
    y = lax.axis_index("y").astype(jnp.int32).reshape(1)
    z = lax.axis_index("z").astype(jnp.int32)
    place = jnp.stack([z, 2 * ((z + lax.axis_index("core").astype(jnp.int32)) % 2) - 1])
    width = weight.shape[1]

    weight_quarter = lax.all_gather(weight, "z", axis=0, tiled=True)
    (sent_two,) = split_inputs(y, lengths, tokens, cotangent, ny, (2,))
    sent_one, sent_three = split_inputs(y, lengths, tokens, cotangent, ny, (1, 3))
    two = swap(sent_two, "y", 2)
    one, three = swap(sent_one, "y", 1), swap(sent_three, "y", 3)

    total, back_two = project_first(y, tokens, two, weight_quarter, ny)
    first = grad_first(y, lengths, tokens, cotangent, two, ny, weight_quarter)
    keep = keep_mask(kept_index)
    terms = grad_terms(place, first, one, three, nz, HALVES, (back_two, keep))
    back_one, back_three = project_rest(one, three, weight_quarter)
    backs = [swap(back_two, "y", 2), swap(back_one, "y", 1), swap(back_three, "y", 3)]

    table = group_table()
    sums, blends = [], []
    for h in range(HALVES):
        last = h == HALVES - 1
        grads = reduce_over_z(*terms[2 * h : 2 * h + 2], (backs[0],) if last else (back_one, back_three))
        after = backs[1:] if last else ()
        blended, coeffs, sent = encode(h * width // HALVES, momentum[0], keep, table, grads, after)
        blends += [blended, coeffs]
        sums += [sent] + [swap(sent, "x", d) for d in (1, 2, 3)]

    projected, projected_token = finish_projection(total, backs)
    new_momentum, new_token = subtract_rebuilt(table, blends, momentum.shape[1:])
    made = ()
    for h in range(HALVES):
        after = (projected_token, new_token) if h == HALVES - 1 else ()
        mine = combine(sums[4 * h : 4 * h + 4], after)
        made = (decode(h, mine, swap(mine, "core", 1), table, width, made),)
    (update,) = made
    return (projected, new_momentum[None], update)


def solution(mesh):
    fine = Mesh(mesh.devices.reshape(4, 2, 4, 8), ("x", "core", "y", "z"))
    rep, fsdp = ("x", "core"), ("y", "z")
    placed = (
        P(rep + fsdp, None),
        P(rep + fsdp, None),
        P(fsdp, None),
        P(rep, fsdp, None),
        P(rep + fsdp),
        P(fsdp, None),
    )
    return jax.shard_map(
        per_device,
        mesh=fine,
        in_specs=placed,
        out_specs=(P(rep + fsdp, None), P(rep, fsdp, None), P(fsdp, None)),
        check_vma=False,
    )
```
